32 devices in a mesh: parts: 2 (over y), dp: 4 (over z), mp: 4 (over x, core).
Axes of the slice: x: 2, y: 2, z: 4, core: 2. Of those that a mesh axis runs over, the one named last changes fastest.
Arguments:
- tokens: bfloat16 [192, 4096], P(('parts', 'dp'), 'mp'), parts along dimension 0, may hold values from -6 to 6
- curvature: float32 [192], P('parts'), parts along dimension 0, may hold values from 0.02 to 0.2
- gate_weight: bfloat16 [4096, 16384], P('mp', 'dp'), may hold values from -0.09375 to 0.09375
- up_weight: bfloat16 [4096, 16384], P('mp', 'dp'), may hold values from -0.09375 to 0.09375
- down_weight: bfloat16 [16384, 4096], P('dp', 'mp'), may hold values from -0.046875 to 0.046875
- gate_vector: bfloat16 [8192, 16384], P(('parts', 'mp'), 'dp'), parts along dimension 0, may hold values from -0.09375 to 0.09375
- up_vector: bfloat16 [8192, 16384], P(('parts', 'mp'), 'dp'), parts along dimension 0, may hold values from -0.09375 to 0.09375
- down_vector: bfloat16 [32768, 4096], P(('parts', 'dp'), 'mp'), parts along dimension 0, may hold values from -0.046875 to 0.046875
Outputs:
- fisher_gate: bfloat16 [8192, 16384], P(('parts', 'mp'), 'dp'), parts along dimension 0
- fisher_up: bfloat16 [8192, 16384], P(('parts', 'mp'), 'dp'), parts along dimension 0
- fisher_down: bfloat16 [32768, 4096], P(('parts', 'dp'), 'mp'), parts along dimension 0
The draws below stay inside these ranges and needn't reach their ends.
There are 2 independent parts, one for each index of `parts`. The reference program is written for one: setup_inputs(seed, part) draws one part's arguments, and reference() takes and returns one part's arrays. A program takes and returns all parts, laid end to end along the dimension named above; an argument that names none is the same for every part. Nothing has to cross between parts.
All inputs are finite; a program needn't handle non-finite values.
Results may differ from the reference program's by a relative error of at most 0.025.
Values may be sent and summed in bfloat16 or wider, within the bound.
No kernel may reach another device: no remote copies, remote signals or barrier semaphores. Data moves between devices by JAX's collectives and lax.ppermute only.
A program may use at most 192 MiB of HBM per device.

```python
import math
import jax
import jax.numpy as jnp
from jax import lax

D = 4096
FF = 16384
TOKENS = 96
N_MP = 4


def steps_of(rng, shape, shards, smallest, high):
    level = 1.0
    for dim, shards_of in shards:
        steps = jax.random.uniform(jax.random.fold_in(jax.random.fold_in(rng, 6), dim), (shards_of,), jnp.float32, smallest / len(shards), high / len(shards))
        level = level * jnp.repeat(jnp.exp(steps), shape[dim] // shards_of).reshape((-1,) + (1,) * (len(shape) - 1 - dim))
    return level


def centred(key, extent, scale, most, cuts=(), kind=jnp.bfloat16):
    result = jax.random.normal(key, extent, jnp.float32) * scale
    if len(cuts) > 0:
        result = steps_of(key, extent, cuts, -0.22, 0.18) * result
    return jnp.clip(result, min=-most, max=most).astype(kind)


def setup_inputs(seed: int = 0, part: int = 0) -> dict:
    seeds = jax.random.split(jax.random.key(seed), 9)
    part_keys = jax.random.split(jax.random.fold_in(seeds[8], part), 9)
    return {
        "tokens": centred(part_keys[0], (TOKENS, D), 1.0, 6.0, ((0, 4), (1, 4))),
        "curvature": jnp.clip(jnp.exp(jax.random.uniform(part_keys[1], (TOKENS,), jnp.float32, math.log(0.02), math.log(0.2))), 0.02, 0.2),
        "gate_weight": centred(seeds[2], (D, FF), D ** -0.5, 0.09375, ((0, 4), (1, 4))),
        "up_weight": centred(seeds[3], (D, FF), D ** -0.5, 0.09375, ((0, 4), (1, 4))),
        "down_weight": centred(seeds[4], (FF, D), FF ** -0.5, 0.046875, ((0, 4), (1, 4))),
        "gate_vector": centred(part_keys[5], (D, FF), D ** -0.5, 0.09375, ((0, 4), (1, 4))),
        "up_vector": centred(part_keys[6], (D, FF), D ** -0.5, 0.09375, ((0, 4), (1, 4))),
        "down_vector": centred(part_keys[7], (FF, D), FF ** -0.5, 0.046875, ((0, 4), (1, 4))),
    }


def block_sums(left, right, blocks):
    width = left.shape[1] // blocks
    total = jnp.zeros((left.shape[0], right.shape[1]), jnp.float32)
    for index in range(blocks):
        product = jnp.dot(left[:, index * width:(index + 1) * width], right[index * width:(index + 1) * width, :], preferred_element_type=jnp.float32)
        rounded = lax.optimization_barrier(product.astype(jnp.bfloat16))
        total = total + rounded.astype(jnp.float32)
    return total


def reference(tokens, curvature, gate_weight, up_weight, down_weight, gate_vector, up_vector, down_vector):
    gate = block_sums(tokens, gate_weight, N_MP)
    up = block_sums(tokens, up_weight, N_MP)
    gate_tan = block_sums(tokens, gate_vector, N_MP)
    up_tan = block_sums(tokens, up_vector, N_MP)
    logistic = jax.nn.sigmoid(gate)
    swish = gate * logistic
    slope = logistic * (1.0 + gate * (1.0 - logistic))
    hidden = (swish * up).astype(jnp.bfloat16)
    hidden_tan = (slope * gate_tan * up + swish * up_tan).astype(jnp.bfloat16)
    out_tan = jnp.dot(hidden_tan, down_weight, preferred_element_type=jnp.float32) + jnp.dot(hidden, down_vector, preferred_element_type=jnp.float32)
    weighted = (curvature[:, None] * out_tan).astype(jnp.bfloat16)
    back = block_sums(weighted, down_weight.T, N_MP)
    gate_back = (back * up * slope).astype(jnp.bfloat16)
    up_back = (back * swish).astype(jnp.bfloat16)
    fisher_gate = jnp.dot(tokens.T, gate_back, preferred_element_type=jnp.float32).astype(jnp.bfloat16)
    fisher_up = jnp.dot(tokens.T, up_back, preferred_element_type=jnp.float32).astype(jnp.bfloat16)
    fisher_down = jnp.dot(hidden.T, weighted, preferred_element_type=jnp.float32).astype(jnp.bfloat16)
    return (fisher_gate, fisher_up, fisher_down)
```

```python
import functools

import jax
import jax.numpy as jnp
from jax import lax
from jax.experimental import pallas as pl
from jax.experimental.pallas import tpu as pltpu
from jax.sharding import PartitionSpec as P

F32, BF16 = jnp.float32, jnp.bfloat16
CHUNKS = 2
PARAMS = pltpu.CompilerParams(vmem_limit_bytes=24 * 1024 * 1024)


def partner(index, step, count):
    if count & (count - 1) == 0:
        return index ^ step
    return (index + step) % count


def giver(index, step, count):
    if count & (count - 1) == 0:
        return index ^ step
    return (index - step) % count


def cost(flops, *arrays):
    return pl.CostEstimate(
        flops=int(flops), bytes_accessed=int(sum(arrays)), transcendentals=0
    )


def call(body, grid, in_specs, out_specs, out_shape, estimate, scratch=(), aliases=None):
    return pl.pallas_call(
        body,
        grid_spec=pltpu.PrefetchScalarGridSpec(
            num_scalar_prefetch=1,
            grid=grid,
            in_specs=in_specs,
            out_specs=out_specs,
            scratch_shapes=scratch,
        ),
        out_shape=out_shape,
        compiler_params=PARAMS,
        cost_estimate=estimate,
        input_output_aliases=aliases or {},
    )


def project(core, rows, weights, side, first, count, added, dtype):
    tokens, depth = rows.shape
    chunk = weights[0].shape[1] // 2 // CHUNKS
    width = min(256, chunk)
    blocks = chunk // width
    kinds = len(weights)

    def body(core_ref, x_ref, *refs):
        for k in range(kinds):
            total = jnp.dot(x_ref[...], refs[k][...], preferred_element_type=F32)
            if added is not None:
                total += refs[kinds][k].astype(F32)
            refs[-1][k] = total.astype(dtype)

    w_spec = pl.BlockSpec(
        (depth, width), lambda j, c: (0, ((c[0] ^ side) * CHUNKS + first) * blocks + j)
    )
    o_spec = pl.BlockSpec((kinds, tokens, width), lambda j, c: (0, 0, j))
    return call(
        body,
        (count * blocks,),
        [pl.BlockSpec((tokens, depth), lambda j, c: (0, 0))]
        + [w_spec] * kinds
        + ([o_spec] if added is not None else []),
        o_spec,
        jax.ShapeDtypeStruct((kinds, tokens, count * chunk), dtype),
        cost(2 * kinds * tokens * depth * chunk * count, 2 * kinds * depth * chunk * count),
    )(core, rows, *weights, *([added] if added is not None else []))


def activate(core, own, others, tangents, index):
    _, tokens, chunk = own.shape
    width = min(512, chunk)
    blocks = chunk // width

    def body(core_ref, own_ref, *refs):
        arrived, t_ref = refs[: len(others)], refs[len(others)]
        hidden_ref, tan_ref, swish_ref, slope_up_ref = refs[len(others) + 1 :]
        gate, up = own_ref[0].astype(F32), own_ref[1].astype(F32)
        for other in arrived:
            gate, up = gate + other[0].astype(F32), up + other[1].astype(F32)
        logistic = jax.nn.sigmoid(gate)
        swish = gate * logistic
        slope_up = logistic * (1.0 + gate * (1.0 - logistic)) * up
        hidden_ref[...] = (swish * up).astype(BF16)
        tan_ref[...] = (slope_up * t_ref[0] + swish * t_ref[1]).astype(BF16)
        swish_ref[...] = swish
        slope_up_ref[...] = slope_up

    pair = pl.BlockSpec((2, tokens, width), lambda j, c: (0, 0, j))
    single = pl.BlockSpec((tokens, width), lambda j, c: (0, j))
    return call(
        body,
        (blocks,),
        [pair] * (1 + len(others))
        + [pl.BlockSpec((2, tokens, width), lambda j, c: (0, 0, index * blocks + j))],
        [single] * 4,
        [jax.ShapeDtypeStruct((tokens, chunk), d) for d in (BF16, BF16, F32, F32)],
        cost(20 * tokens * chunk, 24 * tokens * chunk),
    )(core, own, *others, tangents)


def contract(core, own, other, weight, index, carried, pieces):
    tokens, chunk = own.shape
    width = weight.shape[1]
    deep = min(512, chunk)
    blocks = chunk // deep
    rows = tokens // max(pieces, 1)

    def body(core_ref, own_ref, other_ref, w_ref, *refs):
        total = refs[-1]
        side, k = pl.program_id(0), pl.program_id(1)

        @pl.when((side == 0) & (k == 0))
        def _():
            if carried is None:
                total[...] = jnp.zeros_like(total)
            else:
                total[...] = refs[0][...]

        @pl.when(side == 0)
        def _():
            total[...] += jnp.dot(own_ref[...], w_ref[...], preferred_element_type=F32)

        @pl.when(side == 1)
        def _():
            total[...] += jnp.dot(other_ref[...], w_ref[...], preferred_element_type=F32)

        @pl.when((side == 1) & (k == blocks - 1))
        def _():
            outs = refs[(0 if carried is None else 1) : -1]
            if pieces == 0:
                outs[0][...] = total[...]
            else:
                for p, out in enumerate(outs):
                    out[...] = total[p * rows : (p + 1) * rows, :].astype(out.dtype)

    whole = pl.BlockSpec((tokens, width), lambda s, k, c: (0, 0))
    left = pl.BlockSpec((tokens, deep), lambda s, k, c: (0, k))
    if pieces == 0:
        out_specs, out_shape = whole, jax.ShapeDtypeStruct((tokens, width), F32)
    else:
        out_specs = [pl.BlockSpec((rows, width), lambda s, k, c: (0, 0))] * pieces
        out_shape = [
            jax.ShapeDtypeStruct((rows, width), F32 if p == 0 else BF16) for p in range(pieces)
        ]
    return call(
        body,
        (2, blocks),
        [
            left,
            left,
            pl.BlockSpec(
                (deep, width), lambda s, k, c: (((c[0] ^ s) * CHUNKS + index) * blocks + k, 0)
            ),
        ]
        + ([whole] if carried is not None else []),
        out_specs,
        out_shape,
        cost(4 * tokens * chunk * width, 4 * chunk * width),
        [pltpu.VMEM((tokens, width), F32)],
    )(core, own, other, weight, *([carried] if carried is not None else []))


def pull_back(core, weighted, weight, side, index, added):
    tokens, width = weighted.shape
    chunk = weight.shape[0] // 2 // CHUNKS
    high = min(256, chunk)
    blocks = chunk // high

    def body(core_ref, x_ref, w_ref, *refs):
        total = lax.dot_general(
            x_ref[...], w_ref[...], (((1,), (1,)), ((), ())), preferred_element_type=F32
        )
        if added is not None:
            total += refs[0][...].astype(F32)
        refs[-1][...] = total.astype(BF16)

    spec = pl.BlockSpec((tokens, high), lambda j, c: (0, j))
    return call(
        body,
        (blocks,),
        [
            pl.BlockSpec((tokens, width), lambda j, c: (0, 0)),
            pl.BlockSpec(
                (high, width), lambda j, c: (((c[0] ^ side) * CHUNKS + index) * blocks + j, 0)
            ),
        ]
        + ([spec] if added is not None else []),
        spec,
        jax.ShapeDtypeStruct((tokens, chunk), BF16),
        cost(2 * tokens * chunk * width, 2 * chunk * width),
    )(core, weighted, weight, *([added] if added is not None else []))


def cotangents(core, own, others, swish, slope_up):
    tokens, chunk = own.shape
    width = min(512, chunk)

    def body(core_ref, own_ref, *refs):
        back = own_ref[...].astype(F32)
        for other in refs[: len(others)]:
            back += other[...].astype(F32)
        swish_ref, slope_up_ref, out = refs[len(others) :]
        out[0] = (back * slope_up_ref[...]).astype(BF16)
        out[1] = (back * swish_ref[...]).astype(BF16)

    single = pl.BlockSpec((tokens, width), lambda j, c: (0, j))
    return call(
        body,
        (chunk // width,),
        [single] * (3 + len(others)),
        pl.BlockSpec((2, tokens, width), lambda j, c: (0, 0, j)),
        jax.ShapeDtypeStruct((2, tokens, chunk), BF16),
        cost(4 * tokens * chunk, 16 * tokens * chunk),
    )(core, own, *others, swish, slope_up)


def outer_down(core, hiddens, weighted):
    tokens, chunk = hiddens[0].shape
    width = weighted.shape[1]
    high = min(512, chunk)
    blocks = chunk // high

    def body(core_ref, *refs):
        x_ref, out = refs[-2], refs[-1]
        for m in range(len(hiddens)):

            @pl.when(pl.program_id(0) == m)
            def _(m=m):
                out[...] = lax.dot_general(
                    refs[m][...], x_ref[...], (((0,), (0,)), ((), ())), preferred_element_type=F32
                ).astype(BF16)

    return call(
        body,
        (len(hiddens), blocks),
        [pl.BlockSpec((tokens, high), lambda g, k, c: (0, k))] * len(hiddens)
        + [pl.BlockSpec((tokens, width), lambda g, k, c: (0, 0))],
        pl.BlockSpec(
            (high, width),
            lambda g, k, c: (((c[0] ^ (g // CHUNKS)) * CHUNKS + g % CHUNKS) * blocks + k, 0),
        ),
        jax.ShapeDtypeStruct((len(hiddens) * chunk, width), BF16),
        cost(2 * tokens * len(hiddens) * chunk * width, 2 * len(hiddens) * chunk * width),
    )(core, *hiddens, weighted)


def outer_pair(core, rows, backs, side, index, hidden_units, filled):
    tokens, depth = rows.shape
    chunk = backs.shape[2]
    high = min(256, depth)

    def body(core_ref, x_ref, b_ref, *refs):
        for k in range(2):
            refs[k - 2][...] = lax.dot_general(
                x_ref[...], b_ref[k], (((0,), (0,)), ((), ())), preferred_element_type=F32
            ).astype(BF16)

    return call(
        body,
        (depth // high,),
        [
            pl.BlockSpec((tokens, high), lambda r, c: (0, r)),
            pl.BlockSpec((2, tokens, chunk), lambda r, c: (0, 0, 0)),
        ]
        + ([pl.BlockSpec(memory_space=pl.ANY)] * 2 if filled else []),
        [pl.BlockSpec((high, chunk), lambda r, c: (r, (c[0] ^ side) * CHUNKS + index))] * 2,
        [jax.ShapeDtypeStruct((depth, hidden_units), BF16)] * 2,
        cost(4 * tokens * depth * chunk, 4 * depth * chunk),
        aliases={3: 0, 4: 1} if filled else None,
    )(core, rows, backs, *(filled or ()))


def per_device(
    sizes,
    tokens,
    curvature,
    gate_weight,
    up_weight,
    down_weight,
    gate_vector,
    up_vector,
    down_vector,
):
    groups, chips = sizes["dp"], sizes["mp"] // 2
    hidden_units = gate_weight.shape[1]
    group_rows = tokens.shape[0]
    core = lax.rem(lax.axis_index("mp"), 2).astype(jnp.int32)[None]
    mine = lax.dynamic_slice(curvature, (lax.axis_index("dp") * group_rows,), (group_rows,))

    def over_dp(value, step):
        return lax.ppermute(value, "dp", [(i, partner(i, step, groups)) for i in range(groups)])

    def back_over_dp(value, step):
        return lax.ppermute(value, "dp", [(i, giver(i, step, groups)) for i in range(groups)])

    def to_core(value):
        return lax.ppermute(value, "mp", [(i, i ^ 1) for i in range(2 * chips)])

    def over_chips(value):
        return [
            lax.ppermute(
                value,
                "mp",
                [(2 * i + c, 2 * partner(i, k, chips) + c) for i in range(chips) for c in range(2)],
            )
            for k in range(1, chips)
        ]

    rows = jnp.concatenate([tokens] + [over_dp(tokens, p) for p in range(1, groups)], axis=0)

    primal, probe = (gate_weight, up_weight), (gate_vector, up_vector)
    arrived = [
        to_core(project(core, rows, primal, 1, i, 1, None, BF16)) for i in range(CHUNKS)
    ]
    sums = [project(core, rows, primal, 0, i, 1, arrived[i], BF16) for i in range(CHUNKS)]
    others = [over_chips(s) for s in sums]
    probe_arrived = to_core(project(core, rows, probe, 1, 0, CHUNKS, None, BF16))
    tangents = project(core, rows, probe, 0, 0, CHUNKS, probe_arrived, F32)

    acted = [activate(core, sums[i], others[i], tangents, i) for i in range(CHUNKS)]
    hidden = [a[0] for a in acted]
    hidden_other = [to_core(h) for h in hidden]
    hidden_tan = []
    for a in acted:
        total = a[1].astype(F32)
        for other in over_chips(a[1]):
            total += other.astype(F32)
        hidden_tan.append(total.astype(BF16))
    hidden_tan_other = [to_core(h) for h in hidden_tan]

    carried = None
    for i in range(CHUNKS):
        carried = contract(core, hidden[i], hidden_other[i], down_vector, i, carried, 0)
    for i in range(CHUNKS):
        carried = contract(
            core,
            hidden_tan[i],
            hidden_tan_other[i],
            down_weight,
            i,
            carried,
            groups if i == CHUNKS - 1 else 0,
        )
    out_tan = carried[0]
    for p in range(1, groups):
        out_tan += back_over_dp(carried[p], p).astype(F32)
    weighted_mine = (mine[:, None] * out_tan).astype(BF16)
    weighted = jnp.concatenate(
        [weighted_mine] + [over_dp(weighted_mine, p) for p in range(1, groups)], axis=0
    )

    arrived = [to_core(pull_back(core, weighted, down_weight, 1, i, None)) for i in range(CHUNKS)]
    sums = [pull_back(core, weighted, down_weight, 0, i, arrived[i]) for i in range(CHUNKS)]
    others = [over_chips(s) for s in sums]
    fisher_down = outer_down(core, hidden + hidden_other, weighted)
    filled = None
    for i in range(CHUNKS):
        backs = cotangents(core, sums[i], others[i], acted[i][2], acted[i][3])
        backs_other = to_core(backs)
        filled = outer_pair(core, rows, backs, 0, i, hidden_units, filled)
        filled = outer_pair(core, rows, backs_other, 1, i, hidden_units, filled)
    return (filled[0], filled[1], fisher_down)


def solution(mesh):
    placed = (
        P(("parts", "dp"), "mp"),
        P("parts"),
        P("mp", "dp"),
        P("mp", "dp"),
        P("dp", "mp"),
        P(("parts", "mp"), "dp"),
        P(("parts", "mp"), "dp"),
        P(("parts", "dp"), "mp"),
    )
    return jax.shard_map(
        functools.partial(per_device, dict(mesh.shape)),
        mesh=mesh,
        in_specs=placed,
        out_specs=(P(("parts", "mp"), "dp"), P(("parts", "mp"), "dp"), P(("parts", "dp"), "mp")),
        check_vma=False,
    )
```

```python
import functools

import jax
import jax.numpy as jnp
from jax import lax
from jax.experimental import pallas as pl
from jax.experimental.pallas import tpu as pltpu
from jax.sharding import PartitionSpec as P

F32, BF16 = jnp.float32, jnp.bfloat16
CHUNKS = 2
PIECES = 2
MIB = 1024 * 1024
VMEM = pl.BlockSpec(memory_space=pltpu.VMEM)
SMEM = pl.BlockSpec(memory_space=pltpu.SMEM)
ANY = pl.BlockSpec(memory_space=pl.ANY)
HBM = pl.BlockSpec(memory_space=pltpu.HBM)
ROWS_BY_ROWS = (((0,), (0,)), ((), ()))
COLUMNS_BY_COLUMNS = (((1,), (1,)), ((), ()))


def partner(index, step, count):
    if count & (count - 1) == 0:
        return index ^ step
    return (index + step) % count


def giver(index, step, count):
    if count & (count - 1) == 0:
        return index ^ step
    return (index - step) % count


def shape_of(shape, dtype):
    return jax.ShapeDtypeStruct(shape, dtype)


class Order:
    def __init__(self, core):
        self.core, self.last = core, None


def call(body, order, operands, out_shape, scratch=(), mib=4, out_specs=None, filled=(),
         marked=False):
    after = () if order.last is None else (order.last,)
    idle = len(after) + len(filled)
    plain = [
        pltpu.with_memory_space_constraint(o.array, pltpu.HBM) if isinstance(o, InHbm) else o
        for o in operands
    ]
    single = not isinstance(out_shape, (list, tuple))
    shapes = [out_shape] if single else list(out_shape)
    specs = list(out_specs) if out_specs is not None else [VMEM] * len(shapes)
    if marked:
        shapes, specs = [shape_of((8, 128), F32)] + shapes, [VMEM] + specs

    def kernel(core_ref, *refs):
        outs = refs[len(operands) + idle :]
        if marked:
            outs[0][...] = jnp.zeros((8, 128), F32)
        body(core_ref, *refs[: len(operands)], *outs[marked:])

    outs = pl.pallas_call(
        kernel,
        in_specs=[SMEM]
        + [HBM if isinstance(o, InHbm) else VMEM for o in operands]
        + [ANY] * len(after)
        + [HBM] * len(filled),
        out_specs=specs,
        out_shape=shapes,
        scratch_shapes=scratch,
        compiler_params=pltpu.CompilerParams(vmem_limit_bytes=mib * MIB),
        cost_estimate=pl.CostEstimate(flops=1, bytes_accessed=1, transcendentals=0),
        input_output_aliases={
            1 + len(operands) + len(after) + n: n + marked for n in range(len(filled))
        },
    )(order.core, *plain, *after, *filled)
    order.last = outs[0]
    outs = outs[marked:]
    return outs[0] if single else outs


class InHbm:
    def __init__(self, array):
        self.array = array


def joined(refs):
    return jnp.concatenate([ref[...] for ref in refs], axis=0)


def put(refs, value):
    rows = value.shape[0] // len(refs)
    for p, ref in enumerate(refs):
        ref[...] = value[p * rows : (p + 1) * rows].astype(ref.dtype)


def pieces_of(tokens, width):
    return [shape_of((tokens // PIECES, width), BF16)] * PIECES


def place(core_ref, side, index, chunk):
    return pl.multiple_of(((core_ref[0] ^ side) * CHUNKS + index) * chunk, chunk)


def bring(order, *weights):
    parts = 4

    def body(core_ref, *refs):
        sources, targets, sems = refs[: len(weights)], refs[len(weights) : -1], refs[-1]
        copies = []
        for k in range(len(weights)):
            high = weights[k].shape[0] // parts
            for p in range(parts):
                here = slice(p * high, (p + 1) * high)
                copies.append(
                    pltpu.make_async_copy(
                        sources[k].at[here, :], targets[k].at[here, :], sems.at[k * parts + p]
                    )
                )
                copies[-1].start()
        for copy in copies:
            copy.wait()

    return call(
        body,
        order,
        [InHbm(w) for w in weights],
        [pltpu.VMEM(w.shape, w.dtype) for w in weights],
        scratch=[pltpu.SemaphoreType.DMA((parts * len(weights),))],
        marked=True,
    )


def project(order, rows, weights, side, first, count, added, dtype, pieces=1):
    tokens = rows.shape[0]
    chunk = weights[0].shape[1] // 2 // CHUNKS
    kinds = len(weights)
    high = tokens // pieces

    def body(core_ref, x_ref, *refs):
        arrived, outs = refs[kinds:-pieces], refs[-pieces:]
        for k in range(kinds):
            for i in range(count):
                total = jnp.dot(
                    x_ref[...],
                    refs[k][:, pl.ds(place(core_ref, side, first + i, chunk), chunk)],
                    preferred_element_type=F32,
                )
                here = slice(i * chunk, (i + 1) * chunk)
                if added:
                    total += jnp.concatenate([ref[k, :, here] for ref in arrived], axis=0).astype(F32)
                for p, out in enumerate(outs):
                    out[k, :, here] = total[p * high : (p + 1) * high].astype(dtype)

    return call(
        body,
        order,
        [rows, *weights, *added],
        [shape_of((kinds, high, count * chunk), dtype)] * pieces,
    )


def activate(order, own, others, tangents, index):
    _, tokens, chunk = own.shape
    here = slice(index * chunk, (index + 1) * chunk)

    def body(core_ref, own_ref, *refs):
        arrived, t_ref = refs[: len(others)], refs[len(others)]
        tan_ref, swish_ref, slope_up_ref, *hidden_refs = refs[len(others) + 1 :]
        gate, up = own_ref[0].astype(F32), own_ref[1].astype(F32)
        for other in arrived:
            gate, up = gate + other[0].astype(F32), up + other[1].astype(F32)
        logistic = jax.nn.sigmoid(gate)
        swish = gate * logistic
        slope_up = logistic * (1.0 + gate * (1.0 - logistic)) * up
        put(hidden_refs, swish * up)
        tan_ref[...] = (slope_up * t_ref[0, :, here] + swish * t_ref[1, :, here]).astype(BF16)
        swish_ref[...] = swish
        slope_up_ref[...] = slope_up

    return call(
        body,
        order,
        [own, *others, tangents],
        [shape_of((tokens, chunk), d) for d in (BF16, F32, F32)] + pieces_of(tokens, chunk),
    )


def add_up(order, own, others):
    def body(core_ref, own_ref, *refs):
        total = own_ref[...].astype(F32)
        for other in refs[: len(others)]:
            total += other[...].astype(F32)
        put(refs[len(others) :], total)

    return call(body, order, [own, *others], pieces_of(*own.shape))


def contract(order, terms, weight, carried, groups=0):
    tokens, chunk = terms[0][0][0].shape[0] * PIECES, terms[0][0][0].shape[1]
    width = weight.shape[1]
    rows = tokens // max(groups, 1)
    count = len(terms) * PIECES
    parts = 2
    high = chunk // parts

    def body(core_ref, w_ref, *refs):
        held, sems = refs[-2:]
        copies = []
        for n, (_, side, index) in enumerate(terms):
            start = place(core_ref, side, index, chunk)
            for r in range(parts):
                m = n * parts + r
                here = pl.ds(pl.multiple_of(start + r * high, high), high)
                copies.append(pltpu.make_async_copy(w_ref.at[here, :], held.at[m], sems.at[m]))
                copies[-1].start()
        total = refs[count][...] if carried is not None else None
        for n in range(len(terms)):
            left = joined(refs[n * PIECES : (n + 1) * PIECES])
            for r in range(parts):
                m = n * parts + r
                copies[m].wait()
                term = jnp.dot(
                    left[:, r * high : (r + 1) * high], held[m], preferred_element_type=F32
                )
                total = term if total is None else total + term
        outs = refs[count + (carried is not None) : -2]
        for p, out in enumerate(outs):
            out[...] = total[p * rows : (p + 1) * rows, :].astype(out.dtype)

    out_shape = [shape_of((rows, width), BF16 if p else F32) for p in range(max(groups, 1))]
    outs = call(
        body,
        order,
        [InHbm(weight)]
        + [piece for t in terms for piece in t[0]]
        + ([carried] if carried is not None else []),
        out_shape,
        scratch=[
            pltpu.VMEM((len(terms) * parts, high, width), BF16),
            pltpu.SemaphoreType.DMA((len(terms) * parts,)),
        ],
        mib=4 + 2 * len(terms),
    )
    return outs if groups else outs[0]


def weigh(order, own, others, curvature):
    def body(core_ref, own_ref, *refs):
        total = own_ref[...]
        for other in refs[: len(others)]:
            total += other[...].astype(F32)
        refs[-1][...] = (refs[-2][...] * total).astype(BF16)

    return call(body, order, [own, *others, curvature], shape_of(own.shape, BF16))


def pull_back(order, weighted, weight, side, index, added):
    tokens, width = weighted.shape
    chunk = weight.shape[0] // 2 // CHUNKS

    def body(core_ref, x_ref, w_ref, *refs):
        total = lax.dot_general(
            x_ref[...],
            w_ref[pl.ds(place(core_ref, side, index, chunk), chunk), :],
            COLUMNS_BY_COLUMNS,
            preferred_element_type=F32,
        )
        if added is not None:
            total += refs[0][...].astype(F32)
        refs[-1][...] = total.astype(BF16)

    return call(
        body,
        order,
        [weighted, weight] + ([added] if added is not None else []),
        shape_of((tokens, chunk), BF16),
    )


def cotangents(order, own, others, swish, slope_up):
    def body(core_ref, own_ref, *refs):
        back = own_ref[...].astype(F32)
        for other in refs[: len(others)]:
            back += other[...].astype(F32)
        swish_ref, slope_up_ref, *outs = refs[len(others) :]
        put(outs[:PIECES], back * slope_up_ref[...])
        put(outs[PIECES:], back * swish_ref[...])

    return call(body, order, [own, *others, swish, slope_up], pieces_of(*own.shape) * 2)


def outer_down(order, hiddens, weighted, filled):
    tokens, width = weighted.shape
    chunk = hiddens[0][0][0].shape[1]
    count = len(hiddens)
    high = max(chunk // 4, 16)
    parts = chunk // high

    def body(core_ref, *refs):
        x_ref, out, held, sems = refs[count * PIECES :]
        copies = []
        for m, (_, side, index) in enumerate(hiddens):
            hidden = joined(refs[m * PIECES : (m + 1) * PIECES])
            start = place(core_ref, side, index, chunk)
            for r in range(parts):
                n = m * parts + r
                held[n] = lax.dot_general(
                    hidden[:, r * high : (r + 1) * high],
                    x_ref[...],
                    ROWS_BY_ROWS,
                    preferred_element_type=F32,
                ).astype(BF16)
                there = pl.ds(pl.multiple_of(start + r * high, high), high)
                copies.append(
                    pltpu.make_async_copy(held.at[n], out.at[there, :], sems.at[n])
                )
                copies[-1].start()
        for copy in copies:
            copy.wait()

    return call(
        body,
        order,
        [piece for h in hiddens for piece in h[0]] + [weighted],
        [pltpu.HBM((2 * CHUNKS * chunk, width), BF16)],
        scratch=[
            pltpu.VMEM((count * parts, high, width), BF16),
            pltpu.SemaphoreType.DMA((count * parts,)),
        ],
        mib=12,
        out_specs=[HBM],
        filled=filled,
        marked=True,
    )


def outer_pair(order, rows, terms, hidden_units, filled):
    depth, chunk = rows.shape[1], terms[0][0][0].shape[1]
    high = min(256, depth)
    parts = depth // high
    count = len(terms)

    def body(core_ref, x_ref, *refs):
        *pieces, gate_out, up_out, held, sems = refs
        copies = []
        for t, (_, side, index) in enumerate(terms):
            columns = pl.ds(place(core_ref, side, index, chunk), chunk)
            for k, out in enumerate((gate_out, up_out)):
                n = t * 2 + k
                back = joined(pieces[n * PIECES : (n + 1) * PIECES])
                for r in range(parts):
                    m = n * parts + r
                    held[m] = lax.dot_general(
                        x_ref[:, r * high : (r + 1) * high],
                        back,
                        ROWS_BY_ROWS,
                        preferred_element_type=F32,
                    ).astype(BF16)
                    copies.append(
                        pltpu.make_async_copy(
                            held.at[m], out.at[r * high : (r + 1) * high, columns], sems.at[m]
                        )
                    )
                    copies[-1].start()
        for copy in copies:
            copy.wait()

    return call(
        body,
        order,
        [rows] + [piece for t in terms for piece in t[0]],
        [pltpu.HBM((depth, hidden_units), BF16)] * 2,
        scratch=[
            pltpu.VMEM((2 * count * parts, high, chunk), BF16),
            pltpu.SemaphoreType.DMA((2 * count * parts,)),
        ],
        mib=4 + 4 * count,
        out_specs=[HBM, HBM],
        filled=filled,
        marked=True,
    )


def per_device(
    sizes,
    tokens,
    curvature,
    gate_weight,
    up_weight,
    down_weight,
    gate_vector,
    up_vector,
    down_vector,
):
    groups, chips = sizes["dp"], sizes["mp"] // 2
    hidden_units = gate_weight.shape[1]
    group_rows = tokens.shape[0]
    order = Order(lax.rem(lax.axis_index("mp"), 2).astype(jnp.int32)[None])
    mine = lax.dynamic_slice(curvature, (lax.axis_index("dp") * group_rows,), (group_rows,))[:, None]
    def over_dp(value, step):
        return lax.ppermute(value, "dp", [(i, partner(i, step, groups)) for i in range(groups)])

    def back_over_dp(value, step):
        return lax.ppermute(value, "dp", [(i, giver(i, step, groups)) for i in range(groups)])

    def to_core(value):
        return lax.ppermute(value, "mp", [(i, i ^ 1) for i in range(2 * chips)])

    def over_chips(value):
        return [
            lax.ppermute(
                value,
                "mp",
                [(2 * i + c, 2 * partner(i, k, chips) + c) for i in range(chips) for c in range(2)],
            )
            for k in range(1, chips)
        ]

    primal = bring(order, gate_weight, up_weight)
    rows = jnp.concatenate([tokens] + [over_dp(tokens, p) for p in range(1, groups)], axis=0)
    sent = [project(order, rows, primal, 1, i, 1, [], BF16) for i in range(CHUNKS)]
    sent = [[to_core(piece) for piece in s] for s in sent]
    sums = [project(order, rows, primal, 0, i, 1, sent[i], BF16)[0] for i in range(CHUNKS)]
    others = [over_chips(s) for s in sums]
    probe = bring(order, gate_vector, up_vector)
    sent = [to_core(piece) for piece in project(order, rows, probe, 1, 0, CHUNKS, [], BF16, 3)]
    (tangents,) = project(order, rows, probe, 0, 0, CHUNKS, sent, F32)

    acted = [activate(order, sums[i], others[i], tangents, i) for i in range(CHUNKS)]
    tan_others = [over_chips(a[0]) for a in acted]
    hidden = [(a[3:], 0, i) for i, a in enumerate(acted)]
    hidden_other = [([to_core(piece) for piece in h[0]], 1, h[2]) for h in hidden]
    carried = contract(order, hidden + hidden_other, down_vector, None)
    for i in range(CHUNKS):
        last = i == CHUNKS - 1
        hidden_tan = add_up(order, acted[i][0], tan_others[i])
        tan_other = [to_core(piece) for piece in hidden_tan]
        terms = [(hidden_tan, 0, i), (tan_other, 1, i)]
        if not last:
            carried = contract(order, terms, down_weight, carried)
        else:
            carried = contract(order, terms[:1], down_weight, carried)
            carried = contract(order, terms[1:], down_weight, carried, groups)
    (brought,) = bring(order, down_weight)
    weighted_mine = weigh(
        order, carried[0], [back_over_dp(carried[p], p) for p in range(1, groups)], mine
    )
    weighted = jnp.concatenate(
        [weighted_mine] + [over_dp(weighted_mine, p) for p in range(1, groups)], axis=0
    )

    sent = [to_core(pull_back(order, weighted, brought, 1, i, None)) for i in range(CHUNKS)]
    sums, fisher_down, filled = [], (), ()
    for i in range(CHUNKS):
        sums.append(pull_back(order, weighted, brought, 0, i, sent[i]))
        if i == 0:
            fisher_down = outer_down(order, hidden, weighted, fisher_down)
    fisher_down = outer_down(order, hidden_other, weighted, fisher_down)
    others = [over_chips(s) for s in sums]
    for i in range(CHUNKS):
        backs = cotangents(order, sums[i], others[i], acted[i][1], acted[i][2])
        backs_other = [to_core(piece) for piece in backs]
        terms = [(backs, 0, i), (backs_other, 1, i)]
        if i == 0:
            filled = outer_pair(order, rows, terms, hidden_units, filled)
        else:
            filled = outer_pair(order, rows, terms[:1], hidden_units, filled)
            filled = outer_pair(order, rows, terms[1:], hidden_units, filled)
    return (filled[0], filled[1], fisher_down[0])


def solution(mesh):
    placed = (
        P(("parts", "dp"), "mp"),
        P("parts"),
        P("mp", "dp"),
        P("mp", "dp"),
        P("dp", "mp"),
        P(("parts", "mp"), "dp"),
        P(("parts", "mp"), "dp"),
        P(("parts", "dp"), "mp"),
    )
    return jax.shard_map(
        functools.partial(per_device, dict(mesh.shape)),
        mesh=mesh,
        in_specs=placed,
        out_specs=(P(("parts", "mp"), "dp"), P(("parts", "mp"), "dp"), P(("parts", "dp"), "mp")),
        check_vma=False,
    )
```

```python
import functools

import jax
import jax.numpy as jnp
from jax import lax
from jax.experimental import pallas as pl
from jax.experimental.pallas import tpu as pltpu
from jax.sharding import PartitionSpec as P

F32, BF16 = jnp.float32, jnp.bfloat16
CHUNKS = 2
PIECES = 2
BACK_PIECES = 3
MIB = 1024 * 1024
VMEM = pl.BlockSpec(memory_space=pltpu.VMEM)
SMEM = pl.BlockSpec(memory_space=pltpu.SMEM)
ANY = pl.BlockSpec(memory_space=pl.ANY)
HBM = pl.BlockSpec(memory_space=pltpu.HBM)
ROWS_BY_ROWS = (((0,), (0,)), ((), ()))
COLUMNS_BY_COLUMNS = (((1,), (1,)), ((), ()))


def partner(index, step, count):
    if count & (count - 1) == 0:
        return index ^ step
    return (index + step) % count


def giver(index, step, count):
    if count & (count - 1) == 0:
        return index ^ step
    return (index - step) % count


def shape_of(shape, dtype):
    return jax.ShapeDtypeStruct(shape, dtype)


class Order:
    def __init__(self, core):
        self.core, self.last = core, None


def call(body, order, operands, out_shape, scratch=(), mib=4, out_specs=None, filled=(),
         marked=False):
    after = () if order.last is None else (order.last,)
    idle = len(after) + len(filled)
    plain = [
        pltpu.with_memory_space_constraint(o.array, pltpu.HBM) if isinstance(o, InHbm) else o
        for o in operands
    ]
    single = not isinstance(out_shape, (list, tuple))
    shapes = [out_shape] if single else list(out_shape)
    specs = list(out_specs) if out_specs is not None else [VMEM] * len(shapes)
    if marked:
        shapes, specs = [shape_of((8, 128), F32)] + shapes, [VMEM] + specs

    def kernel(core_ref, *refs):
        outs = refs[len(operands) + idle :]
        if marked:
            outs[0][...] = jnp.zeros((8, 128), F32)
        body(core_ref, *refs[: len(operands)], *outs[marked:])

    outs = pl.pallas_call(
        kernel,
        in_specs=[SMEM]
        + [HBM if isinstance(o, InHbm) else VMEM for o in operands]
        + [ANY] * len(after)
        + [HBM] * len(filled),
        out_specs=specs,
        out_shape=shapes,
        scratch_shapes=scratch,
        compiler_params=pltpu.CompilerParams(vmem_limit_bytes=16 * MIB),
        cost_estimate=pl.CostEstimate(flops=1, bytes_accessed=1, transcendentals=0),
        input_output_aliases={
            1 + len(operands) + len(after) + n: n + marked for n in range(len(filled))
        },
    )(order.core, *plain, *after, *filled)
    order.last = outs[0]
    outs = outs[marked:]
    return outs[0] if single else outs


class InHbm:
    def __init__(self, array):
        self.array = array


def joined(refs):
    return jnp.concatenate([ref[...] for ref in refs], axis=0)


def put(refs, value):
    rows = value.shape[0] // len(refs)
    for p, ref in enumerate(refs):
        ref[...] = value[p * rows : (p + 1) * rows].astype(ref.dtype)


def pieces_of(tokens, width):
    return [shape_of((tokens // PIECES, width), BF16)] * PIECES


def place(core_ref, side, index, chunk):
    return pl.multiple_of(((core_ref[0] ^ side) * CHUNKS + index) * chunk, chunk)


def bring(order, wanted):
    parts = 4
    shapes = []
    for weight, dim, _, _ in wanted:
        shape = list(weight.shape)
        shape[dim] = shape[dim] // 2 // CHUNKS
        shapes.append(tuple(shape))

    def body(core_ref, *refs):
        sources, targets, sems = refs[: len(wanted)], refs[len(wanted) : -1], refs[-1]
        copies = []
        for k, (_, dim, side, index) in enumerate(wanted):
            start = place(core_ref, side, index, shapes[k][dim])
            high = shapes[k][0] // parts
            for p in range(parts):
                here = pl.ds(p * high, high)
                if dim == 0:
                    source = sources[k].at[pl.ds(pl.multiple_of(start + p * high, high), high), :]
                else:
                    source = sources[k].at[here, pl.ds(start, shapes[k][1])]
                copies.append(
                    pltpu.make_async_copy(source, targets[k].at[here, :], sems.at[k * parts + p])
                )
                copies[-1].start()
        for copy in copies:
            copy.wait()

    return call(
        body,
        order,
        [InHbm(w[0]) for w in wanted],
        [pltpu.VMEM(shape, w[0].dtype) for shape, w in zip(shapes, wanted)],
        scratch=[pltpu.SemaphoreType.DMA((parts * len(wanted),))],
        marked=True,
    )


def project(order, rows, weights, added, dtype, pieces=1):
    tokens = rows.shape[0]
    kinds, count = len(weights), len(weights[0])
    chunk = weights[0][0].shape[1]
    high = tokens // pieces

    def body(core_ref, x_ref, *refs):
        arrived, outs = refs[kinds * count : -pieces], refs[-pieces:]
        for k in range(kinds):
            for i in range(count):
                total = jnp.dot(
                    x_ref[...], refs[k * count + i][...], preferred_element_type=F32
                )
                here = slice(i * chunk, (i + 1) * chunk)
                if added:
                    total += jnp.concatenate([ref[k, :, here] for ref in arrived], axis=0).astype(F32)
                for p, out in enumerate(outs):
                    out[k, :, here] = total[p * high : (p + 1) * high].astype(dtype)

    return call(
        body,
        order,
        [rows, *(w for kind in weights for w in kind), *added],
        [shape_of((kinds, high, count * chunk), dtype)] * pieces,
    )


def activate(order, own, others, tangents, index):
    _, tokens, chunk = own.shape
    here = slice(index * chunk, (index + 1) * chunk)

    def body(core_ref, own_ref, *refs):
        arrived, t_ref = refs[: len(others)], refs[len(others)]
        tan_ref, swish_ref, slope_up_ref, *hidden_refs = refs[len(others) + 1 :]
        gate, up = own_ref[0].astype(F32), own_ref[1].astype(F32)
        for other in arrived:
            gate, up = gate + other[0].astype(F32), up + other[1].astype(F32)
        logistic = jax.nn.sigmoid(gate)
        swish = gate * logistic
        slope_up = logistic * (1.0 + gate * (1.0 - logistic)) * up
        put(hidden_refs, swish * up)
        tan_ref[...] = (slope_up * t_ref[0, :, here] + swish * t_ref[1, :, here]).astype(BF16)
        swish_ref[...] = swish
        slope_up_ref[...] = slope_up

    return call(
        body,
        order,
        [own, *others, tangents],
        [shape_of((tokens, chunk), d) for d in (BF16, F32, F32)] + pieces_of(tokens, chunk),
    )


def add_up(order, own, others):
    def body(core_ref, own_ref, *refs):
        total = own_ref[...].astype(F32)
        for other in refs[: len(others)]:
            total += other[...].astype(F32)
        put(refs[len(others) :], total)

    return call(body, order, [own, *others], pieces_of(*own.shape))


def contract(order, terms, weight, carried, groups=0, brought=None):
    tokens, chunk = terms[0][0][0].shape[0] * PIECES, terms[0][0][0].shape[1]
    width = weight.shape[1]
    rows = tokens // max(groups, 1)
    count = len(terms) * PIECES
    parts = 1 if brought else 2
    high = chunk // parts

    def body(core_ref, *refs):
        if brought:
            weights, refs, copies = refs[: len(terms)], refs[len(terms) :], []
        else:
            w_ref, *refs, held, sems = refs
            weights, copies = [held.at[m] for m in range(len(terms) * parts)], []
            for n, (_, side, index) in enumerate(terms):
                start = place(core_ref, side, index, chunk)
                for r in range(parts):
                    m = n * parts + r
                    here = pl.ds(pl.multiple_of(start + r * high, high), high)
                    copies.append(pltpu.make_async_copy(w_ref.at[here, :], held.at[m], sems.at[m]))
                    copies[-1].start()
        total = refs[count][...] if carried is not None else None
        for n in range(len(terms)):
            left = joined(refs[n * PIECES : (n + 1) * PIECES])
            for r in range(parts):
                m = n * parts + r
                if copies:
                    copies[m].wait()
                term = jnp.dot(
                    left[:, r * high : (r + 1) * high], weights[m][...], preferred_element_type=F32
                )
                total = term if total is None else total + term
        outs = refs[count + (carried is not None) :]
        for p, out in enumerate(outs):
            out[...] = total[p * rows : (p + 1) * rows, :].astype(out.dtype)

    out_shape = [shape_of((rows, width), BF16 if p else F32) for p in range(max(groups, 1))]
    outs = call(
        body,
        order,
        (list(brought) if brought else [InHbm(weight)])
        + [piece for t in terms for piece in t[0]]
        + ([carried] if carried is not None else []),
        out_shape,
        scratch=[]
        if brought
        else [
            pltpu.VMEM((len(terms) * parts, high, width), BF16),
            pltpu.SemaphoreType.DMA((len(terms) * parts,)),
        ],
        mib=4 + 2 * len(terms),
    )
    return outs if groups else outs[0]


def weigh(order, own, others, curvature):
    def body(core_ref, own_ref, *refs):
        total = own_ref[...]
        for other in refs[: len(others)]:
            total += other[...].astype(F32)
        refs[-1][...] = (refs[-2][...] * total).astype(BF16)

    return call(body, order, [own, *others, curvature], shape_of(own.shape, BF16))


def pull_back(order, weighted, weight, added):
    def body(core_ref, x_ref, w_ref, *refs):
        total = lax.dot_general(
            x_ref[...], w_ref[...], COLUMNS_BY_COLUMNS, preferred_element_type=F32
        )
        if added is not None:
            total += refs[0][...].astype(F32)
        refs[-1][...] = total.astype(BF16)

    return call(
        body,
        order,
        [weighted, weight] + ([added] if added is not None else []),
        shape_of((weighted.shape[0], weight.shape[0]), BF16),
    )


def cotangents(order, own, others, swish, slope_up):
    tokens, chunk = own.shape
    high = tokens // BACK_PIECES

    def body(core_ref, own_ref, *refs):
        back = own_ref[...].astype(F32)
        for other in refs[: len(others)]:
            back += other[...].astype(F32)
        swish_ref, slope_up_ref, *outs = refs[len(others) :]
        for k, by in enumerate((slope_up_ref, swish_ref)):
            term = (back * by[...]).astype(BF16)
            for p, out in enumerate(outs):
                out[k] = term[p * high : (p + 1) * high]

    return call(
        body,
        order,
        [own, *others, swish, slope_up],
        [shape_of((2, high, chunk), BF16)] * BACK_PIECES,
    )


def outer_down(order, hiddens, weighted, filled):
    tokens, width = weighted.shape
    chunk = hiddens[0][0][0].shape[1]
    count = len(hiddens)
    high = max(chunk // 4, 16)
    parts = chunk // high

    def body(core_ref, *refs):
        x_ref, out, held, sems = refs[count * PIECES :]
        copies = []
        for m, (_, side, index) in enumerate(hiddens):
            hidden = joined(refs[m * PIECES : (m + 1) * PIECES])
            start = place(core_ref, side, index, chunk)
            for r in range(parts):
                n = m * parts + r
                held[n] = lax.dot_general(
                    hidden[:, r * high : (r + 1) * high],
                    x_ref[...],
                    ROWS_BY_ROWS,
                    preferred_element_type=F32,
                ).astype(BF16)
                there = pl.ds(pl.multiple_of(start + r * high, high), high)
                copies.append(
                    pltpu.make_async_copy(held.at[n], out.at[there, :], sems.at[n])
                )
                copies[-1].start()
        for copy in copies:
            copy.wait()

    return call(
        body,
        order,
        [piece for h in hiddens for piece in h[0]] + [weighted],
        [pltpu.HBM((2 * CHUNKS * chunk, width), BF16)],
        scratch=[
            pltpu.VMEM((count * parts, high, width), BF16),
            pltpu.SemaphoreType.DMA((count * parts,)),
        ],
        mib=4 + 2 * count,
        out_specs=[HBM],
        filled=filled,
        marked=True,
    )


def outer_pair(order, rows, terms, hidden_units, filled, marked=True):
    depth, chunk = rows.shape[1], terms[0][0][0].shape[2]
    high = min(256, depth)
    parts = depth // high
    count = len(terms)

    def body(core_ref, x_ref, *refs):
        *pieces, gate_out, up_out, held, sems = refs
        copies = []
        for t, (_, side, index) in enumerate(terms):
            columns = pl.ds(place(core_ref, side, index, chunk), chunk)
            for k, out in enumerate((gate_out, up_out)):
                n = t * 2 + k
                back = jnp.concatenate(
                    [ref[k] for ref in pieces[t * BACK_PIECES : (t + 1) * BACK_PIECES]], axis=0
                )
                for r in range(parts):
                    m = n * parts + r
                    held[m] = lax.dot_general(
                        x_ref[:, r * high : (r + 1) * high],
                        back,
                        ROWS_BY_ROWS,
                        preferred_element_type=F32,
                    ).astype(BF16)
                    copies.append(
                        pltpu.make_async_copy(
                            held.at[m], out.at[r * high : (r + 1) * high, columns], sems.at[m]
                        )
                    )
                    copies[-1].start()
        for copy in copies:
            copy.wait()

    return call(
        body,
        order,
        [rows] + [piece for t in terms for piece in t[0]],
        [pltpu.HBM((depth, hidden_units), BF16)] * 2,
        scratch=[
            pltpu.VMEM((2 * count * parts, high, chunk), BF16),
            pltpu.SemaphoreType.DMA((2 * count * parts,)),
        ],
        mib=6 + 4 * count,
        out_specs=[HBM, HBM],
        filled=filled,
        marked=marked,
    )


def per_device(
    sizes,
    tokens,
    curvature,
    gate_weight,
    up_weight,
    down_weight,
    gate_vector,
    up_vector,
    down_vector,
):
    groups, chips = sizes["dp"], sizes["mp"] // 2
    hidden_units = gate_weight.shape[1]
    group_rows = tokens.shape[0]
    order = Order(lax.rem(lax.axis_index("mp"), 2).astype(jnp.int32)[None])
    mine = lax.dynamic_slice(curvature, (lax.axis_index("dp") * group_rows,), (group_rows,))[:, None]
    def over_dp(value, step):
        return lax.ppermute(value, "dp", [(i, partner(i, step, groups)) for i in range(groups)])

    def back_over_dp(value, step):
        return lax.ppermute(value, "dp", [(i, giver(i, step, groups)) for i in range(groups)])

    def to_core(value):
        return lax.ppermute(value, "mp", [(i, i ^ 1) for i in range(2 * chips)])

    def over_chips(value):
        return [
            lax.ppermute(
                value,
                "mp",
                [(2 * i + c, 2 * partner(i, k, chips) + c) for i in range(chips) for c in range(2)],
            )
            for k in range(1, chips)
        ]

    each = range(CHUNKS)
    own = [[(w, 1, 0, i) for w in (gate_weight, up_weight)] for i in each]
    other = [[(w, 1, 1, i) for w in (gate_weight, up_weight)] for i in each]
    wanted = sum(other, []) + sum(own[:-1], [])
    held = bring(order, wanted)
    rows = jnp.concatenate([tokens] + [over_dp(tokens, p) for p in range(1, groups)], axis=0)

    def pair(n):
        return [[w] for w in held[2 * n : 2 * n + 2]]

    sent = [to_core(project(order, rows, pair(i), [], BF16)[0]) for i in each]
    sums = []
    for i in each:
        if i == CHUNKS - 1:
            held = held + bring(order, own[i])
        sums.append(project(order, rows, pair(CHUNKS + i), [sent[i]], BF16)[0])
    others = [over_chips(s) for s in sums]

    def probes(side):
        held = bring(order, [(w, 1, side, i) for w in (gate_vector, up_vector) for i in each])
        return [held[:CHUNKS], held[CHUNKS:]]

    sent = [to_core(piece) for piece in project(order, rows, probes(1), [], BF16, 3)]
    (tangents,) = project(order, rows, probes(0), sent, F32)

    acted, carried, tan_others = [], None, []
    for i in each:
        acted.append(activate(order, sums[i], others[i], tangents, i))
        tan_others.append(over_chips(acted[i][0]))
        hidden = (acted[i][3:], 0, i)
        hidden_other = ([to_core(piece) for piece in hidden[0]], 1, i)
        carried = contract(order, [hidden, hidden_other], down_vector, carried)
        acted[i] = (*acted[i][:3], hidden, hidden_other)
    for i in each:
        hidden_tan = add_up(order, acted[i][0], tan_others[i])
        tan_other = [to_core(piece) for piece in hidden_tan]
        terms = [(hidden_tan, 0, i), (tan_other, 1, i)]
        if i < CHUNKS - 1:
            carried = contract(order, terms, down_weight, carried)
        else:
            carried = contract(order, terms[:1], down_weight, carried)
            carried = contract(order, terms[1:], down_weight, carried, groups)
    held = bring(order, [(down_weight, 0, side, i) for side in (1, 0) for i in each])
    weighted_mine = weigh(
        order, carried[0], [back_over_dp(carried[p], p) for p in range(1, groups)], mine
    )
    weighted = jnp.concatenate(
        [weighted_mine] + [over_dp(weighted_mine, p) for p in range(1, groups)], axis=0
    )

    sent = [to_core(pull_back(order, weighted, held[i], None)) for i in each]
    sums = [pull_back(order, weighted, held[CHUNKS + i], sent[i]) for i in each]
    others = [over_chips(s) for s in sums]
    (fisher_down,) = outer_down(
        order, [a[3] for a in acted] + [a[4] for a in acted], weighted, ()
    )
    filled, waiting = (), []
    for i in each:
        backs = cotangents(order, sums[i], others[i], acted[i][1], acted[i][2])
        backs_other = [to_core(piece) for piece in backs]
        filled = outer_pair(order, rows, waiting + [(backs, 0, i)], hidden_units, filled)
        waiting = [(backs_other, 1, i)]
    filled = outer_pair(order, rows, waiting, hidden_units, filled, False)
    return (filled[0], filled[1], fisher_down)


def solution(mesh):
    placed = (
        P(("parts", "dp"), "mp"),
        P("parts"),
        P("mp", "dp"),
        P("mp", "dp"),
        P("dp", "mp"),
        P(("parts", "mp"), "dp"),
        P(("parts", "mp"), "dp"),
        P(("parts", "dp"), "mp"),
    )
    return jax.shard_map(
        functools.partial(per_device, dict(mesh.shape)),
        mesh=mesh,
        in_specs=placed,
        out_specs=(P(("parts", "mp"), "dp"), P(("parts", "mp"), "dp"), P(("parts", "dp"), "mp")),
        check_vma=False,
    )
```

```python
import functools

import jax
import jax.numpy as jnp
from jax import lax
from jax.experimental import pallas as pl
from jax.experimental.pallas import tpu as pltpu
from jax.sharding import PartitionSpec as P

F32, BF16 = jnp.float32, jnp.bfloat16
CHUNKS = 2
PIECES = 2
BACK_PIECES = 3
MIB = 1024 * 1024
VMEM = pl.BlockSpec(memory_space=pltpu.VMEM)
SMEM = pl.BlockSpec(memory_space=pltpu.SMEM)
ANY = pl.BlockSpec(memory_space=pl.ANY)
HBM = pl.BlockSpec(memory_space=pltpu.HBM)
ROWS_BY_ROWS = (((0,), (0,)), ((), ()))
COLUMNS_BY_COLUMNS = (((1,), (1,)), ((), ()))


def partner(index, step, count):
    if count & (count - 1) == 0:
        return index ^ step
    return (index + step) % count


def giver(index, step, count):
    if count & (count - 1) == 0:
        return index ^ step
    return (index - step) % count


def shape_of(shape, dtype):
    return jax.ShapeDtypeStruct(shape, dtype)


class Order:
    def __init__(self, core):
        self.core, self.last = core, None


def call(body, order, operands, out_shape, scratch=(), mib=4, out_specs=None, filled=(),
         marked=False):
    after = () if order.last is None else (order.last,)
    idle = len(after) + len(filled)
    plain = [
        pltpu.with_memory_space_constraint(o.array, pltpu.HBM) if isinstance(o, InHbm) else o
        for o in operands
    ]
    single = not isinstance(out_shape, (list, tuple))
    shapes = [out_shape] if single else list(out_shape)
    specs = list(out_specs) if out_specs is not None else [VMEM] * len(shapes)
    if marked:
        shapes, specs = [shape_of((8, 128), F32)] + shapes, [VMEM] + specs

    def kernel(core_ref, *refs):
        outs = refs[len(operands) + idle :]
        if marked:
            outs[0][...] = jnp.zeros((8, 128), F32)
        body(core_ref, *refs[: len(operands)], *outs[marked:])

    outs = pl.pallas_call(
        kernel,
        in_specs=[SMEM]
        + [HBM if isinstance(o, InHbm) else VMEM for o in operands]
        + [ANY] * len(after)
        + [HBM] * len(filled),
        out_specs=specs,
        out_shape=shapes,
        scratch_shapes=scratch,
        compiler_params=pltpu.CompilerParams(vmem_limit_bytes=16 * MIB),
        cost_estimate=pl.CostEstimate(flops=1, bytes_accessed=1, transcendentals=0),
        input_output_aliases={
            1 + len(operands) + len(after) + n: n + marked for n in range(len(filled))
        },
    )(order.core, *plain, *after, *filled)
    order.last = outs[0]
    outs = outs[marked:]
    return outs[0] if single else outs


class InHbm:
    def __init__(self, array):
        self.array = array


def joined(refs):
    return jnp.concatenate([ref[...] for ref in refs], axis=0)


def put(refs, value):
    rows = value.shape[0] // len(refs)
    for p, ref in enumerate(refs):
        ref[...] = value[p * rows : (p + 1) * rows].astype(ref.dtype)


def pieces_of(tokens, width, pieces):
    return [shape_of((tokens // pieces, width), BF16)] * pieces


def place(core_ref, side, index, chunk):
    return pl.multiple_of(((core_ref[0] ^ side) * CHUNKS + index) * chunk, chunk)


def bring(order, wanted):
    parts = 4
    shapes = []
    for weight, dim, _, _ in wanted:
        shape = list(weight.shape)
        shape[dim] = shape[dim] // 2 // CHUNKS
        shapes.append(tuple(shape))

    def body(core_ref, *refs):
        sources, targets, sems = refs[: len(wanted)], refs[len(wanted) : -1], refs[-1]
        copies = []
        for k, (_, dim, side, index) in enumerate(wanted):
            start = place(core_ref, side, index, shapes[k][dim])
            high = shapes[k][0] // parts
            for p in range(parts):
                here = pl.ds(p * high, high)
                if dim == 0:
                    source = sources[k].at[pl.ds(pl.multiple_of(start + p * high, high), high), :]
                else:
                    source = sources[k].at[here, pl.ds(start, shapes[k][1])]
                copies.append(
                    pltpu.make_async_copy(source, targets[k].at[here, :], sems.at[k * parts + p])
                )
                copies[-1].start()
        for copy in copies:
            copy.wait()

    return call(
        body,
        order,
        [InHbm(w[0]) for w in wanted],
        [pltpu.VMEM(shape, w[0].dtype) for shape, w in zip(shapes, wanted)],
        scratch=[pltpu.SemaphoreType.DMA((parts * len(wanted),))],
        marked=True,
    )


def assemble(order, parts):
    tokens = sum(part.shape[0] for part in parts)

    def body(core_ref, *refs):
        rows = jnp.concatenate([ref[...].astype(F32) for ref in refs[:-1]], axis=0)
        refs[-1][...] = rows.astype(BF16)

    return call(body, order, parts, shape_of((tokens, parts[0].shape[1]), BF16))


def project(order, rows, weights, added, dtype, pieces=1, side=0, chunks=()):
    tokens, depth = rows.shape
    kinds, count = len(weights), len(chunks) or len(weights[0])
    chunk = weights[0].shape[1] // 2 // CHUNKS if chunks else weights[0][0].shape[1]
    high = tokens // pieces
    given = kinds if chunks else kinds * count
    parts = 2
    deep = depth // parts

    def body(core_ref, x_ref, *refs):
        copies = []
        if chunks:
            *refs, held, sems = refs
            for k in range(kinds):
                for i, index in enumerate(chunks):
                    columns = pl.ds(place(core_ref, side, index, chunk), chunk)
                    for r in range(parts):
                        m = (k * count + i) * parts + r
                        copies.append(
                            pltpu.make_async_copy(
                                refs[k].at[r * deep : (r + 1) * deep, columns],
                                held.at[k * count + i, r * deep : (r + 1) * deep, :],
                                sems.at[m],
                            )
                        )
                        copies[-1].start()
        arrived, outs = refs[given:-pieces], refs[-pieces:]
        for k in range(kinds):
            for i in range(count):
                n = k * count + i
                for copy in copies[n * parts : (n + 1) * parts]:
                    copy.wait()
                weight = held[n] if chunks else refs[n][...]
                total = jnp.dot(x_ref[...], weight, preferred_element_type=F32)
                here = slice(i * chunk, (i + 1) * chunk)
                if added:
                    total += jnp.concatenate([ref[k, :, here] for ref in arrived], axis=0).astype(F32)
                for p, out in enumerate(outs):
                    out[k, :, here] = total[p * high : (p + 1) * high].astype(dtype)

    return call(
        body,
        order,
        [rows]
        + ([InHbm(w) for w in weights] if chunks else [w for kind in weights for w in kind])
        + list(added),
        [shape_of((kinds, high, count * chunk), dtype)] * pieces,
        scratch=[
            pltpu.VMEM((kinds * count, depth, chunk), BF16),
            pltpu.SemaphoreType.DMA((kinds * count * parts,)),
        ]
        if chunks
        else [],
    )


def activate(order, own, others, tangents, index):
    _, tokens, chunk = own.shape
    here = slice(index * chunk, (index + 1) * chunk)

    def body(core_ref, own_ref, *refs):
        arrived, t_ref = refs[: len(others)], refs[len(others)]
        tan_ref, swish_ref, slope_up_ref, *hidden_refs = refs[len(others) + 1 :]
        gate, up = own_ref[0].astype(F32), own_ref[1].astype(F32)
        for other in arrived:
            gate, up = gate + other[0].astype(F32), up + other[1].astype(F32)
        logistic = jax.nn.sigmoid(gate)
        swish = gate * logistic
        slope_up = logistic * (1.0 + gate * (1.0 - logistic)) * up
        put(hidden_refs, swish * up)
        tan_ref[...] = (slope_up * t_ref[0, :, here] + swish * t_ref[1, :, here]).astype(BF16)
        swish_ref[...] = swish
        slope_up_ref[...] = slope_up

    return call(
        body,
        order,
        [own, *others, tangents],
        [shape_of((tokens, chunk), d) for d in (BF16, F32, F32)] + pieces_of(tokens, chunk, PIECES),
    )


def add_up(order, own, others, pieces):
    def body(core_ref, own_ref, *refs):
        total = own_ref[...].astype(F32)
        for other in refs[: len(others)]:
            total += other[...].astype(F32)
        put(refs[len(others) :], total)

    return call(body, order, [own, *others], pieces_of(*own.shape, pieces))


def contract(order, terms, weight, carried, groups=0):
    pieces = len(terms[0][0])
    tokens, chunk = terms[0][0][0].shape[0] * pieces, terms[0][0][0].shape[1]
    width = weight.shape[1]
    rows = tokens // max(groups, 1)
    count = len(terms) * pieces
    high = min(256, chunk)
    parts = chunk // high

    def body(core_ref, *refs):
        w_ref, *refs, held, sems = refs
        copies = []
        for n, (_, side, index) in enumerate(terms):
            start = place(core_ref, side, index, chunk)
            for r in range(parts):
                m = n * parts + r
                here = pl.ds(pl.multiple_of(start + r * high, high), high)
                copies.append(pltpu.make_async_copy(w_ref.at[here, :], held.at[m], sems.at[m]))
                copies[-1].start()
        total = refs[count][...] if carried is not None else None
        for n in range(len(terms)):
            left = joined(refs[n * pieces : (n + 1) * pieces])
            for r in range(parts):
                m = n * parts + r
                copies[m].wait()
                term = jnp.dot(
                    left[:, r * high : (r + 1) * high], held[m], preferred_element_type=F32
                )
                total = term if total is None else total + term
        outs = refs[count + (carried is not None) :]
        for p, out in enumerate(outs):
            out[...] = total[p * rows : (p + 1) * rows, :].astype(out.dtype)

    out_shape = [shape_of((rows, width), BF16 if p else F32) for p in range(max(groups, 1))]
    outs = call(
        body,
        order,
        [InHbm(weight)]
        + [piece for t in terms for piece in t[0]]
        + ([carried] if carried is not None else []),
        out_shape,
        scratch=[
            pltpu.VMEM((len(terms) * parts, high, width), BF16),
            pltpu.SemaphoreType.DMA((len(terms) * parts,)),
        ],
        mib=4 + 2 * len(terms),
    )
    return outs if groups else outs[0]


def weigh(order, own, others, curvature):
    def body(core_ref, own_ref, *refs):
        total = own_ref[...]
        for other in refs[: len(others)]:
            total += other[...].astype(F32)
        refs[-1][...] = (refs[-2][...] * total).astype(BF16)

    return call(body, order, [own, *others, curvature], shape_of(own.shape, BF16))


def pull_back(order, weighted, weight, added):
    def body(core_ref, x_ref, w_ref, *refs):
        total = lax.dot_general(
            x_ref[...], w_ref[...], COLUMNS_BY_COLUMNS, preferred_element_type=F32
        )
        if added is not None:
            total += refs[0][...].astype(F32)
        refs[-1][...] = total.astype(BF16)

    return call(
        body,
        order,
        [weighted, weight] + ([added] if added is not None else []),
        shape_of((weighted.shape[0], weight.shape[0]), BF16),
    )


def cotangents(order, own, others, swish, slope_up, pieces):
    tokens, chunk = own.shape
    high = tokens // pieces

    def body(core_ref, own_ref, *refs):
        back = own_ref[...].astype(F32)
        for other in refs[: len(others)]:
            back += other[...].astype(F32)
        swish_ref, slope_up_ref, *outs = refs[len(others) :]
        for k, by in enumerate((slope_up_ref, swish_ref)):
            term = (back * by[...]).astype(BF16)
            for p, out in enumerate(outs):
                out[k] = term[p * high : (p + 1) * high]

    return call(
        body,
        order,
        [own, *others, swish, slope_up],
        [shape_of((2, high, chunk), BF16)] * pieces,
    )


def outer_down(order, hiddens, weighted, filled):
    tokens, width = weighted.shape
    chunk = hiddens[0][0][0].shape[1]
    count = len(hiddens)
    high = max(chunk // 4, 16)
    parts = chunk // high

    def body(core_ref, *refs):
        x_ref, out, held, sems = refs[count * PIECES :]
        copies = []
        for m, (_, side, index) in enumerate(hiddens):
            hidden = joined(refs[m * PIECES : (m + 1) * PIECES])
            start = place(core_ref, side, index, chunk)
            for r in range(parts):
                n = m * parts + r
                held[n] = lax.dot_general(
                    hidden[:, r * high : (r + 1) * high],
                    x_ref[...],
                    ROWS_BY_ROWS,
                    preferred_element_type=F32,
                ).astype(BF16)
                there = pl.ds(pl.multiple_of(start + r * high, high), high)
                copies.append(
                    pltpu.make_async_copy(held.at[n], out.at[there, :], sems.at[n])
                )
                copies[-1].start()
        for copy in copies:
            copy.wait()

    return call(
        body,
        order,
        [piece for h in hiddens for piece in h[0]] + [weighted],
        [pltpu.HBM((2 * CHUNKS * chunk, width), BF16)],
        scratch=[
            pltpu.VMEM((count * parts, high, width), BF16),
            pltpu.SemaphoreType.DMA((count * parts,)),
        ],
        mib=4 + 2 * count,
        out_specs=[HBM],
        filled=filled,
        marked=True,
    )


def outer_pair(order, rows, terms, hidden_units, filled, marked=True):
    depth, chunk = rows.shape[1], terms[0][0][0].shape[2]
    high = min(256, depth)
    parts = depth // high
    count = len(terms)

    def body(core_ref, x_ref, *refs):
        *pieces, gate_out, up_out, held, sems = refs
        copies, used = [], 0
        for t, (backs, side, index) in enumerate(terms):
            given, used = pieces[used : used + len(backs)], used + len(backs)
            columns = pl.ds(place(core_ref, side, index, chunk), chunk)
            for k, out in enumerate((gate_out, up_out)):
                n = t * 2 + k
                back = jnp.concatenate([ref[k] for ref in given], axis=0)
                for r in range(parts):
                    m = n * parts + r
                    held[m] = lax.dot_general(
                        x_ref[:, r * high : (r + 1) * high],
                        back,
                        ROWS_BY_ROWS,
                        preferred_element_type=F32,
                    ).astype(BF16)
                    copies.append(
                        pltpu.make_async_copy(
                            held.at[m], out.at[r * high : (r + 1) * high, columns], sems.at[m]
                        )
                    )
                    copies[-1].start()
        for copy in copies:
            copy.wait()

    return call(
        body,
        order,
        [rows] + [piece for t in terms for piece in t[0]],
        [pltpu.HBM((depth, hidden_units), BF16)] * 2,
        scratch=[
            pltpu.VMEM((2 * count * parts, high, chunk), BF16),
            pltpu.SemaphoreType.DMA((2 * count * parts,)),
        ],
        mib=6 + 4 * count,
        out_specs=[HBM, HBM],
        filled=filled,
        marked=marked,
    )


def per_device(
    sizes,
    tokens,
    curvature,
    gate_weight,
    up_weight,
    down_weight,
    gate_vector,
    up_vector,
    down_vector,
):
    groups, chips = sizes["dp"], sizes["mp"] // 2
    hidden_units = gate_weight.shape[1]
    group_rows = tokens.shape[0]
    order = Order(lax.rem(lax.axis_index("mp"), 2).astype(jnp.int32)[None])
    mine = lax.dynamic_slice(curvature, (lax.axis_index("dp") * group_rows,), (group_rows,))[:, None]
    def over_dp(value, step):
        return lax.ppermute(value, "dp", [(i, partner(i, step, groups)) for i in range(groups)])

    def back_over_dp(value, step):
        return lax.ppermute(value, "dp", [(i, giver(i, step, groups)) for i in range(groups)])

    def to_core(value):
        return lax.ppermute(value, "mp", [(i, i ^ 1) for i in range(2 * chips)])

    def over_chips(value):
        return [
            lax.ppermute(
                value,
                "mp",
                [(2 * i + c, 2 * partner(i, k, chips) + c) for i in range(chips) for c in range(2)],
            )
            for k in range(1, chips)
        ]

    each = range(CHUNKS)
    primal, probe = (gate_weight, up_weight), (gate_vector, up_vector)
    wanted = [(w, 1, side, i) for side in (1, 0) for i in each for w in primal]
    held = bring(order, wanted[:-2])
    rows = assemble(order, [tokens] + [over_dp(tokens, p) for p in range(1, groups)])
    sent, sums = [], []
    for n in range(0, len(wanted), 2):
        if n == len(held):
            held += bring(order, wanted[-2:])
        weights = [[w] for w in held[n : n + 2]]
        if n < 2 * CHUNKS:
            sent.append(to_core(project(order, rows, weights, [], BF16)[0]))
        else:
            sums.append(project(order, rows, weights, [sent[len(sums)]], BF16)[0])
    others = [over_chips(s) for s in sums]
    sent = project(order, rows, probe, [], BF16, 3, 1, tuple(each))
    sent = [to_core(piece) for piece in sent]
    held = bring(order, [(w, 1, 0, i) for w in probe for i in each])
    (tangents,) = project(order, rows, [held[:CHUNKS], held[CHUNKS:]], sent, F32)

    acted, carried, tan_others = [], None, []
    for i in each:
        acted.append(activate(order, sums[i], others[i], tangents, i))
        tan_others.append(over_chips(acted[i][0]))
        hidden = (acted[i][3:], 0, i)
        hidden_other = ([to_core(piece) for piece in hidden[0]], 1, i)
        carried = contract(order, [hidden, hidden_other], down_vector, carried)
        acted[i] = (*acted[i][:3], hidden, hidden_other)
    for i in each:
        last = i == CHUNKS - 1
        hidden_tan = add_up(order, acted[i][0], tan_others[i], 1 if last else PIECES)
        tan_other = [to_core(piece) for piece in hidden_tan]
        terms = [(hidden_tan, 0, i), (tan_other, 1, i)]
        if not last:
            carried = contract(order, terms, down_weight, carried)
        else:
            carried = contract(order, terms[:1], down_weight, carried)
            carried = contract(order, terms[1:], down_weight, carried, groups)
    held = bring(order, [(down_weight, 0, 1, i) for i in each])
    weighted_mine = weigh(
        order, carried[0], [back_over_dp(carried[p], p) for p in range(1, groups)], mine
    )
    held += bring(order, [(down_weight, 0, 0, i) for i in each])
    weighted = assemble(
        order, [weighted_mine] + [over_dp(weighted_mine, p) for p in range(1, groups)]
    )

    sent = [to_core(pull_back(order, weighted, held[i], None)) for i in each]
    sums = [pull_back(order, weighted, held[CHUNKS + i], sent[i]) for i in each]
    others = [over_chips(s) for s in sums]
    (fisher_down,) = outer_down(
        order, [a[3] for a in acted] + [a[4] for a in acted], weighted, ()
    )
    filled, waiting = (), []
    for i in each:
        backs = cotangents(order, sums[i], others[i], acted[i][1], acted[i][2], BACK_PIECES)
        backs_other = [to_core(piece) for piece in backs]
        filled = outer_pair(order, rows, waiting + [(backs, 0, i)], hidden_units, filled)
        waiting = [(backs_other, 1, i)]
    filled = outer_pair(order, rows, waiting, hidden_units, filled, False)
    return (filled[0], filled[1], fisher_down)


def solution(mesh):
    placed = (
        P(("parts", "dp"), "mp"),
        P("parts"),
        P("mp", "dp"),
        P("mp", "dp"),
        P("dp", "mp"),
        P(("parts", "mp"), "dp"),
        P(("parts", "mp"), "dp"),
        P(("parts", "dp"), "mp"),
    )
    return jax.shard_map(
        functools.partial(per_device, dict(mesh.shape)),
        mesh=mesh,
        in_specs=placed,
        out_specs=(P(("parts", "mp"), "dp"), P(("parts", "mp"), "dp"), P(("parts", "dp"), "mp")),
        check_vma=False,
    )
```

```python
import functools

import jax
import jax.numpy as jnp
from jax import lax
from jax.experimental import pallas as pl
from jax.experimental.pallas import tpu as pltpu
from jax.sharding import PartitionSpec as P

F32, BF16 = jnp.float32, jnp.bfloat16
CHUNKS = 2
PIECES = 2
BACK_PIECES = 3
MIB = 1024 * 1024
VMEM = pl.BlockSpec(memory_space=pltpu.VMEM)
SMEM = pl.BlockSpec(memory_space=pltpu.SMEM)
ANY = pl.BlockSpec(memory_space=pl.ANY)
HBM = pl.BlockSpec(memory_space=pltpu.HBM)
ROWS_BY_ROWS = (((0,), (0,)), ((), ()))
COLUMNS_BY_COLUMNS = (((1,), (1,)), ((), ()))


def partner(index, step, count):
    if count & (count - 1) == 0:
        return index ^ step
    return (index + step) % count


def giver(index, step, count):
    if count & (count - 1) == 0:
        return index ^ step
    return (index - step) % count


def shape_of(shape, dtype):
    return jax.ShapeDtypeStruct(shape, dtype)


class Order:
    def __init__(self, core):
        self.core, self.last = core, None


def call(body, order, operands, out_shape, scratch=(), mib=4, out_specs=None, filled=(),
         marked=False):
    after = () if order.last is None else (order.last,)
    idle = len(after) + len(filled)
    plain = [
        pltpu.with_memory_space_constraint(o.array, pltpu.HBM) if isinstance(o, InHbm) else o
        for o in operands
    ]
    single = not isinstance(out_shape, (list, tuple))
    shapes = [out_shape] if single else list(out_shape)
    specs = list(out_specs) if out_specs is not None else [VMEM] * len(shapes)
    if marked:
        shapes, specs = [shape_of((8, 128), F32)] + shapes, [VMEM] + specs

    def kernel(core_ref, *refs):
        outs = refs[len(operands) + idle :]
        if marked:
            outs[0][...] = jnp.zeros((8, 128), F32)
        body(core_ref, *refs[: len(operands)], *outs[marked:])

    outs = pl.pallas_call(
        kernel,
        in_specs=[SMEM]
        + [HBM if isinstance(o, InHbm) else VMEM for o in operands]
        + [ANY] * len(after)
        + [HBM] * len(filled),
        out_specs=specs,
        out_shape=shapes,
        scratch_shapes=scratch,
        compiler_params=pltpu.CompilerParams(vmem_limit_bytes=16 * MIB),
        cost_estimate=pl.CostEstimate(flops=1, bytes_accessed=1, transcendentals=0),
        input_output_aliases={
            1 + len(operands) + len(after) + n: n + marked for n in range(len(filled))
        },
    )(order.core, *plain, *after, *filled)
    order.last = outs[0]
    outs = outs[marked:]
    return outs[0] if single else outs


class InHbm:
    def __init__(self, array):
        self.array = array


def joined(refs):
    return jnp.concatenate([ref[...] for ref in refs], axis=0)


def put(refs, value):
    rows = value.shape[0] // len(refs)
    for p, ref in enumerate(refs):
        ref[...] = value[p * rows : (p + 1) * rows].astype(ref.dtype)


def pieces_of(tokens, width, pieces):
    return [shape_of((tokens // pieces, width), BF16)] * pieces


def place(core_ref, side, index, chunk):
    return pl.multiple_of(((core_ref[0] ^ side) * CHUNKS + index) * chunk, chunk)


def bring(order, wanted):
    parts = 4
    shapes = []
    for weight, dim, _, _ in wanted:
        shape = list(weight.shape)
        shape[dim] = shape[dim] // 2 // CHUNKS
        shapes.append(tuple(shape))

    def body(core_ref, *refs):
        sources, targets, sems = refs[: len(wanted)], refs[len(wanted) : -1], refs[-1]
        copies = []
        for k, (_, dim, side, index) in enumerate(wanted):
            start = place(core_ref, side, index, shapes[k][dim])
            high = shapes[k][0] // parts
            for p in range(parts):
                here = pl.ds(p * high, high)
                if dim == 0:
                    source = sources[k].at[pl.ds(pl.multiple_of(start + p * high, high), high), :]
                else:
                    source = sources[k].at[here, pl.ds(start, shapes[k][1])]
                copies.append(
                    pltpu.make_async_copy(source, targets[k].at[here, :], sems.at[k * parts + p])
                )
                copies[-1].start()
        for copy in copies:
            copy.wait()

    return call(
        body,
        order,
        [InHbm(w[0]) for w in wanted],
        [pltpu.VMEM(shape, w[0].dtype) for shape, w in zip(shapes, wanted)],
        scratch=[pltpu.SemaphoreType.DMA((parts * len(wanted),))],
        marked=True,
    )


def assemble(order, parts):
    tokens = sum(part.shape[0] for part in parts)

    def body(core_ref, *refs):
        rows = jnp.concatenate([ref[...].astype(F32) for ref in refs[:-1]], axis=0)
        refs[-1][...] = rows.astype(BF16)

    return call(body, order, parts, shape_of((tokens, parts[0].shape[1]), BF16))


def project(order, rows, weights, added, dtype, pieces=1, side=0, chunks=()):
    tokens, depth = rows.shape
    kinds, count = len(weights), len(chunks) or len(weights[0])
    chunk = weights[0].shape[1] // 2 // CHUNKS if chunks else weights[0][0].shape[1]
    high = tokens // pieces
    given = kinds if chunks else kinds * count
    parts = 2
    deep = depth // parts

    def body(core_ref, x_ref, *refs):
        copies = []
        if chunks:
            *refs, held, sems = refs
            for k in range(kinds):
                for i, index in enumerate(chunks):
                    columns = pl.ds(place(core_ref, side, index, chunk), chunk)
                    for r in range(parts):
                        m = (k * count + i) * parts + r
                        copies.append(
                            pltpu.make_async_copy(
                                refs[k].at[r * deep : (r + 1) * deep, columns],
                                held.at[k * count + i, r * deep : (r + 1) * deep, :],
                                sems.at[m],
                            )
                        )
                        copies[-1].start()
        arrived, outs = refs[given:-pieces], refs[-pieces:]
        for k in range(kinds):
            for i in range(count):
                n = k * count + i
                for copy in copies[n * parts : (n + 1) * parts]:
                    copy.wait()
                weight = held[n] if chunks else refs[n][...]
                total = jnp.dot(x_ref[...], weight, preferred_element_type=F32)
                here = slice(i * chunk, (i + 1) * chunk)
                if added:
                    total += jnp.concatenate([ref[k, :, here] for ref in arrived], axis=0).astype(F32)
                for p, out in enumerate(outs):
                    out[k, :, here] = total[p * high : (p + 1) * high].astype(dtype)

    return call(
        body,
        order,
        [rows]
        + ([InHbm(w) for w in weights] if chunks else [w for kind in weights for w in kind])
        + list(added),
        [shape_of((kinds, high, count * chunk), dtype)] * pieces,
        scratch=[
            pltpu.VMEM((kinds * count, depth, chunk), BF16),
            pltpu.SemaphoreType.DMA((kinds * count * parts,)),
        ]
        if chunks
        else [],
    )


def activate(order, own, others, tangents, index):
    _, tokens, chunk = own.shape
    here = slice(index * chunk, (index + 1) * chunk)

    def body(core_ref, own_ref, *refs):
        arrived, t_ref = refs[: len(others)], refs[len(others)]
        tan_ref, swish_ref, slope_up_ref, *hidden_refs = refs[len(others) + 1 :]
        gate, up = own_ref[0].astype(F32), own_ref[1].astype(F32)
        for other in arrived:
            gate, up = gate + other[0].astype(F32), up + other[1].astype(F32)
        logistic = jax.nn.sigmoid(gate)
        swish = gate * logistic
        slope_up = logistic * (1.0 + gate * (1.0 - logistic)) * up
        put(hidden_refs, swish * up)
        tan_ref[...] = (slope_up * t_ref[0, :, here] + swish * t_ref[1, :, here]).astype(BF16)
        swish_ref[...] = swish
        slope_up_ref[...] = slope_up

    return call(
        body,
        order,
        [own, *others, tangents],
        [shape_of((tokens, chunk), d) for d in (BF16, F32, F32)] + pieces_of(tokens, chunk, PIECES),
    )


def add_up(order, own, others, pieces):
    def body(core_ref, own_ref, *refs):
        total = own_ref[...].astype(F32)
        for other in refs[: len(others)]:
            total += other[...].astype(F32)
        put(refs[len(others) :], total)

    return call(body, order, [own, *others], pieces_of(*own.shape, pieces))


def contract(order, terms, weight, carried, groups=0, brought=(), ahead=()):
    pieces = len(terms[0][0])
    tokens, chunk = terms[0][0][0].shape[0] * pieces, terms[0][0][0].shape[1]
    width = weight.shape[1]
    rows = tokens // max(groups, 1)
    count = len(terms) * pieces
    high = min(256, chunk)
    parts = chunk // high
    wanted = ([] if brought else [t[1:] for t in terms]) + [a[1:] for a in ahead]
    streamed = len(wanted) - len(ahead)
    given = len(brought) or 1
    results = max(groups, 1)

    def body(core_ref, *refs):
        w_refs, next_refs, refs = refs[:given], refs[given:][: len(ahead)], refs[given + len(ahead) :]
        copies = []
        if wanted:
            *refs, sems = refs
            if streamed:
                *refs, held = refs
            for n, (side, index) in enumerate(wanted):
                start = place(core_ref, side, index, chunk)
                for r in range(parts):
                    m = n * parts + r
                    here = pl.ds(pl.multiple_of(start + r * high, high), high)
                    if n < streamed:
                        source, target = w_refs[0], held.at[m]
                    else:
                        source = next_refs[n - streamed]
                        target = refs[n - len(wanted)].at[r * high : (r + 1) * high, :]
                    copies.append(pltpu.make_async_copy(source.at[here, :], target, sems.at[m]))
                    copies[-1].start()
        total = refs[count][...] if carried is not None else None
        for n in range(len(terms)):
            left = joined(refs[n * pieces : (n + 1) * pieces])
            for r in range(parts):
                here = slice(r * high, (r + 1) * high)
                if brought:
                    right = w_refs[n][here, :]
                else:
                    copies[n * parts + r].wait()
                    right = held[n * parts + r]
                term = jnp.dot(left[:, here], right, preferred_element_type=F32)
                total = term if total is None else total + term
        outs = refs[count + (carried is not None) :][:results]
        for p, out in enumerate(outs):
            out[...] = total[p * rows : (p + 1) * rows, :].astype(out.dtype)
        for copy in copies[streamed * parts :]:
            copy.wait()

    out_shape = [shape_of((rows, width), BF16 if p else F32) for p in range(results)]
    outs = call(
        body,
        order,
        (list(brought) or [InHbm(weight)])
        + [InHbm(a[0]) for a in ahead]
        + [piece for t in terms for piece in t[0]]
        + ([carried] if carried is not None else []),
        out_shape + [pltpu.VMEM((chunk, width), weight.dtype) for _ in ahead],
        scratch=([pltpu.VMEM((streamed * parts, high, width), BF16)] if streamed else [])
        + ([pltpu.SemaphoreType.DMA((len(wanted) * parts,))] if wanted else []),
    )
    return outs[:results] if groups else outs[0], outs[results:]


def weigh(order, own, others, curvature):
    def body(core_ref, own_ref, *refs):
        total = own_ref[...]
        for other in refs[: len(others)]:
            total += other[...].astype(F32)
        refs[-1][...] = (refs[-2][...] * total).astype(BF16)

    return call(body, order, [own, *others, curvature], shape_of(own.shape, BF16))


def pull_back(order, weighted, weight, added):
    def body(core_ref, x_ref, w_ref, *refs):
        total = lax.dot_general(
            x_ref[...], w_ref[...], COLUMNS_BY_COLUMNS, preferred_element_type=F32
        )
        if added is not None:
            total += refs[0][...].astype(F32)
        refs[-1][...] = total.astype(BF16)

    return call(
        body,
        order,
        [weighted, weight] + ([added] if added is not None else []),
        shape_of((weighted.shape[0], weight.shape[0]), BF16),
    )


def cotangents(order, own, others, swish, slope_up, pieces):
    tokens, chunk = own.shape
    high = tokens // pieces

    def body(core_ref, own_ref, *refs):
        back = own_ref[...].astype(F32)
        for other in refs[: len(others)]:
            back += other[...].astype(F32)
        swish_ref, slope_up_ref, *outs = refs[len(others) :]
        for k, by in enumerate((slope_up_ref, swish_ref)):
            term = (back * by[...]).astype(BF16)
            for p, out in enumerate(outs):
                out[k] = term[p * high : (p + 1) * high]

    return call(
        body,
        order,
        [own, *others, swish, slope_up],
        [shape_of((2, high, chunk), BF16)] * pieces,
    )


def outer_down(order, hiddens, weighted, filled):
    tokens, width = weighted.shape
    chunk = hiddens[0][0][0].shape[1]
    count = len(hiddens)
    high = max(chunk // 4, 16)
    parts = chunk // high

    def body(core_ref, *refs):
        x_ref, out, held, sems = refs[count * PIECES :]
        copies = []
        for m, (_, side, index) in enumerate(hiddens):
            hidden = joined(refs[m * PIECES : (m + 1) * PIECES])
            start = place(core_ref, side, index, chunk)
            for r in range(parts):
                n = m * parts + r
                held[n] = lax.dot_general(
                    hidden[:, r * high : (r + 1) * high],
                    x_ref[...],
                    ROWS_BY_ROWS,
                    preferred_element_type=F32,
                ).astype(BF16)
                there = pl.ds(pl.multiple_of(start + r * high, high), high)
                copies.append(
                    pltpu.make_async_copy(held.at[n], out.at[there, :], sems.at[n])
                )
                copies[-1].start()
        for copy in copies:
            copy.wait()

    return call(
        body,
        order,
        [piece for h in hiddens for piece in h[0]] + [weighted],
        [pltpu.HBM((2 * CHUNKS * chunk, width), BF16)],
        scratch=[
            pltpu.VMEM((count * parts, high, width), BF16),
            pltpu.SemaphoreType.DMA((count * parts,)),
        ],
        mib=4 + 2 * count,
        out_specs=[HBM],
        filled=filled,
        marked=True,
    )


def outer_pair(order, rows, terms, hidden_units, filled, marked=True):
    depth, chunk = rows.shape[1], terms[0][0][0].shape[2]
    high = min(256, depth)
    parts = depth // high
    count = len(terms)

    def body(core_ref, x_ref, *refs):
        *pieces, gate_out, up_out, held, sems = refs
        copies, used = [], 0
        for t, (backs, side, index) in enumerate(terms):
            given, used = pieces[used : used + len(backs)], used + len(backs)
            columns = pl.ds(place(core_ref, side, index, chunk), chunk)
            for k, out in enumerate((gate_out, up_out)):
                n = t * 2 + k
                back = jnp.concatenate([ref[k] for ref in given], axis=0)
                for r in range(parts):
                    m = n * parts + r
                    held[m] = lax.dot_general(
                        x_ref[:, r * high : (r + 1) * high],
                        back,
                        ROWS_BY_ROWS,
                        preferred_element_type=F32,
                    ).astype(BF16)
                    copies.append(
                        pltpu.make_async_copy(
                            held.at[m], out.at[r * high : (r + 1) * high, columns], sems.at[m]
                        )
                    )
                    copies[-1].start()
        for copy in copies:
            copy.wait()

    return call(
        body,
        order,
        [rows] + [piece for t in terms for piece in t[0]],
        [pltpu.HBM((depth, hidden_units), BF16)] * 2,
        scratch=[
            pltpu.VMEM((2 * count * parts, high, chunk), BF16),
            pltpu.SemaphoreType.DMA((2 * count * parts,)),
        ],
        mib=6 + 4 * count,
        out_specs=[HBM, HBM],
        filled=filled,
        marked=marked,
    )


def per_device(
    sizes,
    tokens,
    curvature,
    gate_weight,
    up_weight,
    down_weight,
    gate_vector,
    up_vector,
    down_vector,
):
    groups, chips = sizes["dp"], sizes["mp"] // 2
    hidden_units = gate_weight.shape[1]
    group_rows = tokens.shape[0]
    order = Order(lax.rem(lax.axis_index("mp"), 2).astype(jnp.int32)[None])
    mine = lax.dynamic_slice(curvature, (lax.axis_index("dp") * group_rows,), (group_rows,))[:, None]
    def over_dp(value, step):
        return lax.ppermute(value, "dp", [(i, partner(i, step, groups)) for i in range(groups)])

    def back_over_dp(value, step):
        return lax.ppermute(value, "dp", [(i, giver(i, step, groups)) for i in range(groups)])

    def to_core(value):
        return lax.ppermute(value, "mp", [(i, i ^ 1) for i in range(2 * chips)])

    def over_chips(value):
        return [
            lax.ppermute(
                value,
                "mp",
                [(2 * i + c, 2 * partner(i, k, chips) + c) for i in range(chips) for c in range(2)],
            )
            for k in range(1, chips)
        ]

    each = range(CHUNKS)
    primal, probe = (gate_weight, up_weight), (gate_vector, up_vector)
    wanted = [(w, 1, side, i) for side in (1, 0) for i in each for w in primal]
    held = bring(order, wanted[:-2])
    rows = assemble(order, [tokens] + [over_dp(tokens, p) for p in range(1, groups)])
    sent, sums = [], []
    for n in range(0, len(wanted), 2):
        if n == len(held):
            held += bring(order, wanted[-2:])
        weights = [[w] for w in held[n : n + 2]]
        if n < 2 * CHUNKS:
            sent.append(to_core(project(order, rows, weights, [], BF16)[0]))
        else:
            sums.append(project(order, rows, weights, [sent[len(sums)]], BF16)[0])
    others = [over_chips(s) for s in sums]
    sent = project(order, rows, probe, [], BF16, 3, 1, tuple(each))
    sent = [to_core(piece) for piece in sent]
    held = bring(order, [(w, 1, 0, i) for w in probe for i in each])
    (tangents,) = project(order, rows, [held[:CHUNKS], held[CHUNKS:]], sent, F32)

    acted, carried, tan_others, brought = [], None, [], ()
    for i in each:
        acted.append(activate(order, sums[i], others[i], tangents, i))
        tan_others.append(over_chips(acted[i][0]))
        hidden = (acted[i][3:], 0, i)
        hidden_other = ([to_core(piece) for piece in hidden[0]], 1, i)
        if i < CHUNKS - 1:
            ahead = [(down_vector, side, i + 1) for side in (0, 1)]
        else:
            ahead = [(down_weight, side, 0) for side in (0, 1)]
        carried, brought = contract(
            order, [hidden, hidden_other], down_vector, carried, 0, brought, ahead
        )
        acted[i] = (*acted[i][:3], hidden, hidden_other)
    for i in each:
        last = i == CHUNKS - 1
        hidden_tan = add_up(order, acted[i][0], tan_others[i], 1 if last else PIECES)
        tan_other = [to_core(piece) for piece in hidden_tan]
        terms = [(hidden_tan, 0, i), (tan_other, 1, i)]
        if not last:
            ahead = [(down_weight, 0, i + 1)] if False else []
            carried, brought = contract(order, terms, down_weight, carried, 0, brought, ahead)
        else:
            carried, brought = contract(
                order, terms[:1], down_weight, carried, 0, brought, [(down_weight, 1, i)]
            )
            carried, _ = contract(order, terms[1:], down_weight, carried, groups, brought)
    held = bring(order, [(down_weight, 0, 1, i) for i in each])
    weighted_mine = weigh(
        order, carried[0], [back_over_dp(carried[p], p) for p in range(1, groups)], mine
    )
    held += bring(order, [(down_weight, 0, 0, i) for i in each])
    weighted = assemble(
        order, [weighted_mine] + [over_dp(weighted_mine, p) for p in range(1, groups)]
    )

    sent = [to_core(pull_back(order, weighted, held[i], None)) for i in each]
    sums = [pull_back(order, weighted, held[CHUNKS + i], sent[i]) for i in each]
    others = [over_chips(s) for s in sums]
    (fisher_down,) = outer_down(
        order, [a[3] for a in acted] + [a[4] for a in acted], weighted, ()
    )
    filled, waiting = (), []
    for i in each:
        backs = cotangents(order, sums[i], others[i], acted[i][1], acted[i][2], BACK_PIECES)
        backs_other = [to_core(piece) for piece in backs]
        filled = outer_pair(order, rows, waiting + [(backs, 0, i)], hidden_units, filled)
        waiting = [(backs_other, 1, i)]
    filled = outer_pair(order, rows, waiting, hidden_units, filled, False)
    return (filled[0], filled[1], fisher_down)


def solution(mesh):
    placed = (
        P(("parts", "dp"), "mp"),
        P("parts"),
        P("mp", "dp"),
        P("mp", "dp"),
        P("dp", "mp"),
        P(("parts", "mp"), "dp"),
        P(("parts", "mp"), "dp"),
        P(("parts", "dp"), "mp"),
    )
    return jax.shard_map(
        functools.partial(per_device, dict(mesh.shape)),
        mesh=mesh,
        in_specs=placed,
        out_specs=(P(("parts", "mp"), "dp"), P(("parts", "mp"), "dp"), P(("parts", "dp"), "mp")),
        check_vma=False,
    )
```

```python
import functools

import jax
import jax.numpy as jnp
from jax import lax
from jax.experimental import pallas as pl
from jax.experimental.pallas import tpu as pltpu
from jax.sharding import PartitionSpec as P

F32, BF16 = jnp.float32, jnp.bfloat16
CHUNKS = 2
PIECES = 2
BACK_PIECES = 3
MIB = 1024 * 1024
VMEM = pl.BlockSpec(memory_space=pltpu.VMEM)
SMEM = pl.BlockSpec(memory_space=pltpu.SMEM)
ANY = pl.BlockSpec(memory_space=pl.ANY)
HBM = pl.BlockSpec(memory_space=pltpu.HBM)
ROWS_BY_ROWS = (((0,), (0,)), ((), ()))
COLUMNS_BY_COLUMNS = (((1,), (1,)), ((), ()))


def partner(index, step, count):
    if count & (count - 1) == 0:
        return index ^ step
    return (index + step) % count


def giver(index, step, count):
    if count & (count - 1) == 0:
        return index ^ step
    return (index - step) % count


def shape_of(shape, dtype):
    return jax.ShapeDtypeStruct(shape, dtype)


class Order:
    def __init__(self, core):
        self.core, self.last = core, None


def call(body, order, operands, out_shape, scratch=(), mib=4, out_specs=None, filled=(),
         marked=False):
    after = () if order.last is None else (order.last,)
    idle = len(after) + len(filled)
    plain = [
        pltpu.with_memory_space_constraint(o.array, pltpu.HBM) if isinstance(o, InHbm) else o
        for o in operands
    ]
    single = not isinstance(out_shape, (list, tuple))
    shapes = [out_shape] if single else list(out_shape)
    specs = list(out_specs) if out_specs is not None else [VMEM] * len(shapes)
    if marked:
        shapes, specs = [shape_of((8, 128), F32)] + shapes, [VMEM] + specs

    def kernel(core_ref, *refs):
        outs = refs[len(operands) + idle :]
        if marked:
            outs[0][...] = jnp.zeros((8, 128), F32)
        body(core_ref, *refs[: len(operands)], *outs[marked:])

    outs = pl.pallas_call(
        kernel,
        in_specs=[SMEM]
        + [HBM if isinstance(o, InHbm) else VMEM for o in operands]
        + [ANY] * len(after)
        + [HBM] * len(filled),
        out_specs=specs,
        out_shape=shapes,
        scratch_shapes=scratch,
        compiler_params=pltpu.CompilerParams(vmem_limit_bytes=16 * MIB),
        cost_estimate=pl.CostEstimate(flops=1, bytes_accessed=1, transcendentals=0),
        input_output_aliases={
            1 + len(operands) + len(after) + n: n + marked for n in range(len(filled))
        },
    )(order.core, *plain, *after, *filled)
    order.last = outs[0]
    outs = outs[marked:]
    return outs[0] if single else outs


class InHbm:
    def __init__(self, array):
        self.array = array


def joined(refs):
    return jnp.concatenate([ref[...] for ref in refs], axis=0)


def put(refs, value):
    rows = value.shape[0] // len(refs)
    for p, ref in enumerate(refs):
        ref[...] = value[p * rows : (p + 1) * rows].astype(ref.dtype)


def pieces_of(tokens, width, pieces):
    return [shape_of((tokens // pieces, width), BF16)] * pieces


def place(core_ref, side, index, chunk):
    return pl.multiple_of(((core_ref[0] ^ side) * CHUNKS + index) * chunk, chunk)


def bring(order, wanted):
    parts = 1
    shapes = []
    for weight, dim, _, _ in wanted:
        shape = list(weight.shape)
        shape[dim] = shape[dim] // 2 // CHUNKS
        shapes.append(tuple(shape))

    def body(core_ref, *refs):
        sources, targets, sems = refs[: len(wanted)], refs[len(wanted) : -1], refs[-1]
        copies = []
        for k, (_, dim, side, index) in enumerate(wanted):
            start = place(core_ref, side, index, shapes[k][dim])
            high = shapes[k][0] // parts
            for p in range(parts):
                here = pl.ds(p * high, high)
                if dim == 0:
                    source = sources[k].at[pl.ds(pl.multiple_of(start + p * high, high), high), :]
                else:
                    source = sources[k].at[here, pl.ds(start, shapes[k][1])]
                copies.append(
                    pltpu.make_async_copy(source, targets[k].at[here, :], sems.at[k * parts + p])
                )
                copies[-1].start()
        for copy in copies:
            copy.wait()

    return call(
        body,
        order,
        [InHbm(w[0]) for w in wanted],
        [pltpu.VMEM(shape, w[0].dtype) for shape, w in zip(shapes, wanted)],
        scratch=[pltpu.SemaphoreType.DMA((parts * len(wanted),))],
        marked=True,
    )


def assemble(order, parts):
    tokens = sum(part.shape[0] for part in parts)

    def body(core_ref, *refs):
        rows = jnp.concatenate([ref[...].astype(F32) for ref in refs[:-1]], axis=0)
        refs[-1][...] = rows.astype(BF16)

    return call(body, order, parts, shape_of((tokens, parts[0].shape[1]), BF16))


def project(order, rows, weights, added, dtype, pieces=1, side=0, chunks=()):
    tokens, depth = rows.shape
    kinds, count = len(weights), len(chunks) or len(weights[0])
    chunk = weights[0].shape[1] // 2 // CHUNKS if chunks else weights[0][0].shape[1]
    high = tokens // pieces
    given = kinds if chunks else kinds * count
    parts = 4
    deep = depth // parts

    def body(core_ref, x_ref, *refs):
        copies = []
        if chunks:
            *refs, held, sems = refs
            for k in range(kinds):
                for i, index in enumerate(chunks):
                    columns = pl.ds(place(core_ref, side, index, chunk), chunk)
                    for r in range(parts):
                        m = (k * count + i) * parts + r
                        copies.append(
                            pltpu.make_async_copy(
                                refs[k].at[r * deep : (r + 1) * deep, columns],
                                held.at[k * count + i, r * deep : (r + 1) * deep, :],
                                sems.at[m],
                            )
                        )
                        copies[-1].start()
        arrived, outs = refs[given:-pieces], refs[-pieces:]
        for k in range(kinds):
            for i in range(count):
                n = k * count + i
                for copy in copies[n * parts : (n + 1) * parts]:
                    copy.wait()
                weight = held[n] if chunks else refs[n][...]
                total = jnp.dot(x_ref[...], weight, preferred_element_type=F32)
                here = slice(i * chunk, (i + 1) * chunk)
                if added:
                    total += jnp.concatenate([ref[k, :, here] for ref in arrived], axis=0).astype(F32)
                for p, out in enumerate(outs):
                    out[k, :, here] = total[p * high : (p + 1) * high].astype(dtype)

    return call(
        body,
        order,
        [rows]
        + ([InHbm(w) for w in weights] if chunks else [w for kind in weights for w in kind])
        + list(added),
        [shape_of((kinds, high, count * chunk), dtype)] * pieces,
        scratch=[
            pltpu.VMEM((kinds * count, depth, chunk), BF16),
            pltpu.SemaphoreType.DMA((kinds * count * parts,)),
        ]
        if chunks
        else [],
    )


def activate(order, own, others, tangents, index):
    _, tokens, chunk = own.shape
    here = slice(index * chunk, (index + 1) * chunk)

    def body(core_ref, own_ref, *refs):
        arrived, t_ref = refs[: len(others)], refs[len(others)]
        tan_ref, swish_ref, slope_up_ref, *hidden_refs = refs[len(others) + 1 :]
        gate, up = own_ref[0].astype(F32), own_ref[1].astype(F32)
        for other in arrived:
            gate, up = gate + other[0].astype(F32), up + other[1].astype(F32)
        logistic = jax.nn.sigmoid(gate)
        swish = gate * logistic
        slope_up = logistic * (1.0 + gate * (1.0 - logistic)) * up
        put(hidden_refs, swish * up)
        tan_ref[...] = (slope_up * t_ref[0, :, here] + swish * t_ref[1, :, here]).astype(BF16)
        swish_ref[...] = swish
        slope_up_ref[...] = slope_up

    return call(
        body,
        order,
        [own, *others, tangents],
        [shape_of((tokens, chunk), d) for d in (BF16, F32, F32)] + pieces_of(tokens, chunk, PIECES),
    )


def add_up(order, own, others, pieces):
    def body(core_ref, own_ref, *refs):
        total = own_ref[...].astype(F32)
        for other in refs[: len(others)]:
            total += other[...].astype(F32)
        put(refs[len(others) :], total)

    return call(body, order, [own, *others], pieces_of(*own.shape, pieces))


def settle(order, kept, arrived):
    def body(core_ref, kept_ref, arrived_ref, out):
        out[...] = (kept_ref[...] + arrived_ref[...].astype(F32)).astype(BF16)

    return call(body, order, [kept, arrived], shape_of(kept.shape, BF16))


def contract(order, terms, weight, carried, groups=0, brought=(), ahead=()):
    pieces = len(terms[0][0])
    tokens, chunk = terms[0][0][0].shape[0] * pieces, terms[0][0][0].shape[1]
    width = weight.shape[1]
    rows = tokens // max(groups, 1)
    count = len(terms) * pieces
    high = min(256, chunk)
    parts = chunk // high
    wanted = ([] if brought else [t[1:] for t in terms]) + [a[1:] for a in ahead]
    streamed = len(wanted) - len(ahead)
    given = len(brought) or 1
    results = max(groups, 1)

    def body(core_ref, *refs):
        w_refs, next_refs, refs = refs[:given], refs[given:][: len(ahead)], refs[given + len(ahead) :]
        copies = []
        if wanted:
            *refs, sems = refs
            if streamed:
                *refs, held = refs
            for n, (side, index) in enumerate(wanted):
                start = place(core_ref, side, index, chunk)
                for r in range(parts):
                    m = n * parts + r
                    here = pl.ds(pl.multiple_of(start + r * high, high), high)
                    if n < streamed:
                        source, target = w_refs[0], held.at[m]
                    else:
                        source = next_refs[n - streamed]
                        target = refs[n - len(wanted)].at[r * high : (r + 1) * high, :]
                    copies.append(pltpu.make_async_copy(source.at[here, :], target, sems.at[m]))
                    copies[-1].start()
        total = refs[count][...] if carried is not None else None
        for n in range(len(terms)):
            left = joined(refs[n * pieces : (n + 1) * pieces])
            for r in range(parts):
                here = slice(r * high, (r + 1) * high)
                if brought:
                    right = w_refs[n][here, :]
                else:
                    copies[n * parts + r].wait()
                    right = held[n * parts + r]
                term = jnp.dot(left[:, here], right, preferred_element_type=F32)
                total = term if total is None else total + term
        outs = refs[count + (carried is not None) :][:results]
        for p, out in enumerate(outs):
            out[...] = total[p * rows : (p + 1) * rows, :].astype(out.dtype)
        for copy in copies[streamed * parts :]:
            copy.wait()

    out_shape = [shape_of((rows, width), BF16 if p else F32) for p in range(results)]
    outs = call(
        body,
        order,
        (list(brought) or [InHbm(weight)])
        + [InHbm(a[0]) for a in ahead]
        + [piece for t in terms for piece in t[0]]
        + ([carried] if carried is not None else []),
        out_shape + [pltpu.VMEM((chunk, width), weight.dtype) for _ in ahead],
        scratch=([pltpu.VMEM((streamed * parts, high, width), BF16)] if streamed else [])
        + ([pltpu.SemaphoreType.DMA((len(wanted) * parts,))] if wanted else []),
    )
    return outs[:results] if groups else outs[0], outs[results:]


def weigh(order, own, others, curvature):
    def body(core_ref, own_ref, *refs):
        total = own_ref[...]
        for other in refs[: len(others)]:
            total += other[...].astype(F32)
        refs[-1][...] = (refs[-2][...] * total).astype(BF16)

    return call(body, order, [own, *others, curvature], shape_of(own.shape, BF16))


def pull_back(order, weighted, weight, added, dtype=BF16):
    def body(core_ref, x_ref, w_ref, *refs):
        total = lax.dot_general(
            x_ref[...], w_ref[...], COLUMNS_BY_COLUMNS, preferred_element_type=F32
        )
        if added is not None:
            total += refs[0][...].astype(F32)
        refs[-1][...] = total.astype(dtype)

    return call(
        body,
        order,
        [weighted, weight] + ([added] if added is not None else []),
        shape_of((weighted.shape[0], weight.shape[0]), dtype),
    )


def cotangents(order, own, others, swish, slope_up, pieces):
    tokens, chunk = own.shape
    high = tokens // pieces

    def body(core_ref, own_ref, *refs):
        back = own_ref[...].astype(F32)
        for other in refs[: len(others)]:
            back += other[...].astype(F32)
        swish_ref, slope_up_ref, *outs = refs[len(others) :]
        for k, by in enumerate((slope_up_ref, swish_ref)):
            term = (back * by[...]).astype(BF16)
            for p, out in enumerate(outs):
                out[k] = term[p * high : (p + 1) * high]

    return call(
        body,
        order,
        [own, *others, swish, slope_up],
        [shape_of((2, high, chunk), BF16)] * pieces,
    )


def outer_down(order, hiddens, weighted, filled):
    tokens, width = weighted.shape
    chunk = hiddens[0][0][0].shape[1]
    count = len(hiddens)
    high = max(chunk // 4, 16)
    parts = chunk // high

    def body(core_ref, *refs):
        x_ref, out, held, sems = refs[count * PIECES :]
        copies = []
        for m, (_, side, index) in enumerate(hiddens):
            hidden = joined(refs[m * PIECES : (m + 1) * PIECES])
            start = place(core_ref, side, index, chunk)
            for r in range(parts):
                n = m * parts + r
                held[n] = lax.dot_general(
                    hidden[:, r * high : (r + 1) * high],
                    x_ref[...],
                    ROWS_BY_ROWS,
                    preferred_element_type=F32,
                ).astype(BF16)
                there = pl.ds(pl.multiple_of(start + r * high, high), high)
                copies.append(
                    pltpu.make_async_copy(held.at[n], out.at[there, :], sems.at[n])
                )
                copies[-1].start()
        for copy in copies:
            copy.wait()

    return call(
        body,
        order,
        [piece for h in hiddens for piece in h[0]] + [weighted],
        [pltpu.HBM((2 * CHUNKS * chunk, width), BF16)],
        scratch=[
            pltpu.VMEM((count * parts, high, width), BF16),
            pltpu.SemaphoreType.DMA((count * parts,)),
        ],
        mib=4 + 2 * count,
        out_specs=[HBM],
        filled=filled,
        marked=True,
    )


def outer_pair(order, rows, terms, hidden_units, filled, marked=True):
    depth, chunk = rows.shape[1], terms[0][0][0].shape[2]
    high = min(256, depth)
    parts = depth // high
    count = len(terms)

    def body(core_ref, x_ref, *refs):
        *pieces, gate_out, up_out, held, sems = refs
        copies, used = [], 0
        for t, (backs, side, index) in enumerate(terms):
            given, used = pieces[used : used + len(backs)], used + len(backs)
            columns = pl.ds(place(core_ref, side, index, chunk), chunk)
            for k, out in enumerate((gate_out, up_out)):
                n = t * 2 + k
                back = jnp.concatenate([ref[k] for ref in given], axis=0)
                for r in range(parts):
                    m = n * parts + r
                    held[m] = lax.dot_general(
                        x_ref[:, r * high : (r + 1) * high],
                        back,
                        ROWS_BY_ROWS,
                        preferred_element_type=F32,
                    ).astype(BF16)
                    copies.append(
                        pltpu.make_async_copy(
                            held.at[m], out.at[r * high : (r + 1) * high, columns], sems.at[m]
                        )
                    )
                    copies[-1].start()
        for copy in copies:
            copy.wait()

    return call(
        body,
        order,
        [rows] + [piece for t in terms for piece in t[0]],
        [pltpu.HBM((depth, hidden_units), BF16)] * 2,
        scratch=[
            pltpu.VMEM((2 * count * parts, high, chunk), BF16),
            pltpu.SemaphoreType.DMA((2 * count * parts,)),
        ],
        mib=6 + 4 * count,
        out_specs=[HBM, HBM],
        filled=filled,
        marked=marked,
    )


def per_device(
    sizes,
    tokens,
    curvature,
    gate_weight,
    up_weight,
    down_weight,
    gate_vector,
    up_vector,
    down_vector,
):
    groups, chips = sizes["dp"], sizes["mp"] // 2
    hidden_units = gate_weight.shape[1]
    group_rows = tokens.shape[0]
    order = Order(lax.rem(lax.axis_index("mp"), 2).astype(jnp.int32)[None])
    mine = lax.dynamic_slice(curvature, (lax.axis_index("dp") * group_rows,), (group_rows,))[:, None]
    def over_dp(value, step):
        return lax.ppermute(value, "dp", [(i, partner(i, step, groups)) for i in range(groups)])

    def back_over_dp(value, step):
        return lax.ppermute(value, "dp", [(i, giver(i, step, groups)) for i in range(groups)])

    def to_core(value):
        return lax.ppermute(value, "mp", [(i, i ^ 1) for i in range(2 * chips)])

    def over_chips(value):
        return [
            lax.ppermute(
                value,
                "mp",
                [(2 * i + c, 2 * partner(i, k, chips) + c) for i in range(chips) for c in range(2)],
            )
            for k in range(1, chips)
        ]

    each = range(CHUNKS)
    primal, probe = (gate_weight, up_weight), (gate_vector, up_vector)
    wanted = [(w, 1, side, i) for side in (1, 0) for i in each for w in primal]
    held = bring(order, wanted[:-2])
    rows = assemble(order, [tokens] + [over_dp(tokens, p) for p in range(1, groups)])
    sent, sums = [], []
    for n in range(0, len(wanted), 2):
        if n == len(held):
            held += bring(order, wanted[-2:])
        weights = [[w] for w in held[n : n + 2]]
        if n < 2 * CHUNKS:
            sent.append(to_core(project(order, rows, weights, [], BF16)[0]))
        else:
            i = len(sums)
            if i == 0:
                (kept,) = project(order, rows, weights, [], F32)
                sums.append(settle(order, kept, sent[i]))
            else:
                sums.append(project(order, rows, weights, [sent[i]], BF16)[0])
    others = [over_chips(s) for s in sums]
    sent = project(order, rows, probe, [], BF16, 3, 1, tuple(each))
    sent = [to_core(piece) for piece in sent]
    held = bring(order, [(w, 1, 0, i) for w in probe for i in each])
    (tangents,) = project(order, rows, [held[:CHUNKS], held[CHUNKS:]], sent, F32)

    acted, carried, tan_others, brought = [], None, [], ()
    for i in each:
        acted.append(activate(order, sums[i], others[i], tangents, i))
        tan_others.append(over_chips(acted[i][0]))
        hidden = (acted[i][3:], 0, i)
        hidden_other = ([to_core(piece) for piece in hidden[0]], 1, i)
        if i < CHUNKS - 1:
            ahead = [(down_vector, side, i + 1) for side in (0, 1)]
        else:
            ahead = [(down_weight, side, 0) for side in (0, 1)]
        carried, brought = contract(
            order, [hidden, hidden_other], down_vector, carried, 0, brought, ahead
        )
        acted[i] = (*acted[i][:3], hidden, hidden_other)
    for i in each:
        last = i == CHUNKS - 1
        hidden_tan = add_up(order, acted[i][0], tan_others[i], 1 if last else PIECES)
        tan_other = [to_core(piece) for piece in hidden_tan]
        terms = [(hidden_tan, 0, i), (tan_other, 1, i)]
        if not last:
            ahead = [(down_weight, 0, i + 1)] if False else []
            carried, brought = contract(order, terms, down_weight, carried, 0, brought, ahead)
        else:
            carried, brought = contract(
                order, terms[:1], down_weight, carried, 0, brought, [(down_weight, 1, i)]
            )
            carried, _ = contract(order, terms[1:], down_weight, carried, groups, brought)
    held = bring(order, [(down_weight, 0, 1, i) for i in each])
    weighted_mine = weigh(
        order, carried[0], [back_over_dp(carried[p], p) for p in range(1, groups)], mine
    )
    held += bring(order, [(down_weight, 0, 0, i) for i in each])
    weighted = assemble(
        order, [weighted_mine] + [over_dp(weighted_mine, p) for p in range(1, groups)]
    )

    sent = [to_core(pull_back(order, weighted, held[i], None)) for i in each]
    kept = pull_back(order, weighted, held[CHUNKS], None, F32)
    sums = [settle(order, kept, sent[0])]
    sums += [pull_back(order, weighted, held[CHUNKS + i], sent[i]) for i in each[1:]]
    others = [over_chips(s) for s in sums]
    (fisher_down,) = outer_down(
        order, [a[3] for a in acted] + [a[4] for a in acted], weighted, ()
    )
    filled, waiting = (), []
    for i in each:
        backs = cotangents(order, sums[i], others[i], acted[i][1], acted[i][2], BACK_PIECES)
        backs_other = [to_core(piece) for piece in backs]
        filled = outer_pair(order, rows, waiting + [(backs, 0, i)], hidden_units, filled)
        waiting = [(backs_other, 1, i)]
    filled = outer_pair(order, rows, waiting, hidden_units, filled, False)
    return (filled[0], filled[1], fisher_down)


def solution(mesh):
    placed = (
        P(("parts", "dp"), "mp"),
        P("parts"),
        P("mp", "dp"),
        P("mp", "dp"),
        P("dp", "mp"),
        P(("parts", "mp"), "dp"),
        P(("parts", "mp"), "dp"),
        P(("parts", "dp"), "mp"),
    )
    return jax.shard_map(
        functools.partial(per_device, dict(mesh.shape)),
        mesh=mesh,
        in_specs=placed,
        out_specs=(P(("parts", "mp"), "dp"), P(("parts", "mp"), "dp"), P(("parts", "dp"), "mp")),
        check_vma=False,
    )
```

```python
import functools

import jax
import jax.numpy as jnp
from jax import lax
from jax.experimental import pallas as pl
from jax.experimental.pallas import tpu as pltpu
from jax.sharding import PartitionSpec as P

F32, BF16 = jnp.float32, jnp.bfloat16
CHUNKS = 2
PIECES = 2
BACK_PIECES = 3
MIB = 1024 * 1024
VMEM = pl.BlockSpec(memory_space=pltpu.VMEM)
SMEM = pl.BlockSpec(memory_space=pltpu.SMEM)
ANY = pl.BlockSpec(memory_space=pl.ANY)
HBM = pl.BlockSpec(memory_space=pltpu.HBM)
ROWS_BY_ROWS = (((0,), (0,)), ((), ()))
COLUMNS_BY_COLUMNS = (((1,), (1,)), ((), ()))


def partner(index, step, count):
    if count & (count - 1) == 0:
        return index ^ step
    return (index + step) % count


def giver(index, step, count):
    if count & (count - 1) == 0:
        return index ^ step
    return (index - step) % count


def shape_of(shape, dtype):
    return jax.ShapeDtypeStruct(shape, dtype)


class Order:
    def __init__(self, core):
        self.core, self.last = core, None


def call(body, order, operands, out_shape, scratch=(), mib=4, out_specs=None, filled=(),
         marked=False):
    after = () if order.last is None else (order.last,)
    idle = len(after) + len(filled)
    plain = [
        pltpu.with_memory_space_constraint(o.array, pltpu.HBM) if isinstance(o, InHbm) else o
        for o in operands
    ]
    single = not isinstance(out_shape, (list, tuple))
    shapes = [out_shape] if single else list(out_shape)
    specs = list(out_specs) if out_specs is not None else [VMEM] * len(shapes)
    if marked:
        shapes, specs = [shape_of((8, 128), F32)] + shapes, [VMEM] + specs

    def kernel(core_ref, *refs):
        outs = refs[len(operands) + idle :]
        if marked:
            outs[0][...] = jnp.zeros((8, 128), F32)
        body(core_ref, *refs[: len(operands)], *outs[marked:])

    outs = pl.pallas_call(
        kernel,
        in_specs=[SMEM]
        + [HBM if isinstance(o, InHbm) else VMEM for o in operands]
        + [ANY] * len(after)
        + [HBM] * len(filled),
        out_specs=specs,
        out_shape=shapes,
        scratch_shapes=scratch,
        compiler_params=pltpu.CompilerParams(vmem_limit_bytes=16 * MIB),
        cost_estimate=pl.CostEstimate(flops=1, bytes_accessed=1, transcendentals=0),
        input_output_aliases={
            1 + len(operands) + len(after) + n: n + marked for n in range(len(filled))
        },
    )(order.core, *plain, *after, *filled)
    order.last = outs[0]
    outs = outs[marked:]
    return outs[0] if single else outs


class InHbm:
    def __init__(self, array):
        self.array = array


def joined(refs):
    return jnp.concatenate([ref[...] for ref in refs], axis=0)


def put(refs, value):
    rows = value.shape[0] // len(refs)
    for p, ref in enumerate(refs):
        ref[...] = value[p * rows : (p + 1) * rows].astype(ref.dtype)


def pieces_of(tokens, width, pieces):
    return [shape_of((tokens // pieces, width), BF16)] * pieces


def place(core_ref, side, index, chunk):
    return pl.multiple_of(((core_ref[0] ^ side) * CHUNKS + index) * chunk, chunk)


def bring(order, wanted):
    parts = 1
    shapes = []
    for weight, dim, _, _ in wanted:
        shape = list(weight.shape)
        shape[dim] = shape[dim] // 2 // CHUNKS
        shapes.append(tuple(shape))

    def body(core_ref, *refs):
        sources, targets, sems = refs[: len(wanted)], refs[len(wanted) : -1], refs[-1]
        copies = []
        for k, (_, dim, side, index) in enumerate(wanted):
            start = place(core_ref, side, index, shapes[k][dim])
            high = shapes[k][0] // parts
            for p in range(parts):
                here = pl.ds(p * high, high)
                if dim == 0:
                    source = sources[k].at[pl.ds(pl.multiple_of(start + p * high, high), high), :]
                else:
                    source = sources[k].at[here, pl.ds(start, shapes[k][1])]
                copies.append(
                    pltpu.make_async_copy(source, targets[k].at[here, :], sems.at[k * parts + p])
                )
                copies[-1].start()
        for copy in copies:
            copy.wait()

    return call(
        body,
        order,
        [InHbm(w[0]) for w in wanted],
        [pltpu.VMEM(shape, w[0].dtype) for shape, w in zip(shapes, wanted)],
        scratch=[pltpu.SemaphoreType.DMA((parts * len(wanted),))],
        marked=True,
    )


def assemble(order, parts):
    tokens = sum(part.shape[0] for part in parts)

    def body(core_ref, *refs):
        rows = jnp.concatenate([ref[...].astype(F32) for ref in refs[:-1]], axis=0)
        refs[-1][...] = rows.astype(BF16)

    return call(body, order, parts, shape_of((tokens, parts[0].shape[1]), BF16))


def project(order, rows, weights, added, dtype, pieces=1, side=0, chunks=()):
    tokens, depth = rows.shape
    kinds, count = len(weights), len(chunks) or len(weights[0])
    chunk = weights[0].shape[1] // 2 // CHUNKS if chunks else weights[0][0].shape[1]
    high = tokens // pieces
    given = kinds if chunks else kinds * count
    parts = 4
    deep = depth // parts

    def body(core_ref, x_ref, *refs):
        copies = []
        if chunks:
            *refs, held, sems = refs
            for k in range(kinds):
                for i, index in enumerate(chunks):
                    columns = pl.ds(place(core_ref, side, index, chunk), chunk)
                    for r in range(parts):
                        m = (k * count + i) * parts + r
                        copies.append(
                            pltpu.make_async_copy(
                                refs[k].at[r * deep : (r + 1) * deep, columns],
                                held.at[k * count + i, r * deep : (r + 1) * deep, :],
                                sems.at[m],
                            )
                        )
                        copies[-1].start()
        arrived, outs = refs[given:-pieces], refs[-pieces:]
        for k in range(kinds):
            for i in range(count):
                n = k * count + i
                for copy in copies[n * parts : (n + 1) * parts]:
                    copy.wait()
                weight = held[n] if chunks else refs[n][...]
                total = jnp.dot(x_ref[...], weight, preferred_element_type=F32)
                here = slice(i * chunk, (i + 1) * chunk)
                if added:
                    total += jnp.concatenate([ref[k, :, here] for ref in arrived], axis=0).astype(F32)
                for p, out in enumerate(outs):
                    out[k, :, here] = total[p * high : (p + 1) * high].astype(dtype)

    return call(
        body,
        order,
        [rows]
        + ([InHbm(w) for w in weights] if chunks else [w for kind in weights for w in kind])
        + list(added),
        [shape_of((kinds, high, count * chunk), dtype)] * pieces,
        scratch=[
            pltpu.VMEM((kinds * count, depth, chunk), BF16),
            pltpu.SemaphoreType.DMA((kinds * count * parts,)),
        ]
        if chunks
        else [],
    )


def activate(order, own, others, tangents, index):
    _, tokens, chunk = own.shape
    here = slice(index * chunk, (index + 1) * chunk)

    def body(core_ref, own_ref, *refs):
        arrived, t_ref = refs[: len(others)], refs[len(others)]
        tan_ref, swish_ref, slope_up_ref, *hidden_refs = refs[len(others) + 1 :]
        gate, up = own_ref[0].astype(F32), own_ref[1].astype(F32)
        for other in arrived:
            gate, up = gate + other[0].astype(F32), up + other[1].astype(F32)
        logistic = jax.nn.sigmoid(gate)
        swish = gate * logistic
        slope_up = logistic * (1.0 + gate * (1.0 - logistic)) * up
        put(hidden_refs, swish * up)
        tan_ref[...] = (slope_up * t_ref[0, :, here] + swish * t_ref[1, :, here]).astype(BF16)
        swish_ref[...] = swish
        slope_up_ref[...] = slope_up

    return call(
        body,
        order,
        [own, *others, tangents],
        [shape_of((tokens, chunk), d) for d in (BF16, F32, F32)] + pieces_of(tokens, chunk, PIECES),
    )


def add_up(order, own, others, pieces):
    def body(core_ref, own_ref, *refs):
        total = own_ref[...].astype(F32)
        for other in refs[: len(others)]:
            total += other[...].astype(F32)
        put(refs[len(others) :], total)

    return call(body, order, [own, *others], pieces_of(*own.shape, pieces))


def settle(order, kept, arrived):
    def body(core_ref, kept_ref, arrived_ref, out):
        out[...] = (kept_ref[...] + arrived_ref[...].astype(F32)).astype(BF16)

    return call(body, order, [kept, arrived], shape_of(kept.shape, BF16))


def contract(order, terms, weight, carried, groups=0, brought=(), ahead=()):
    pieces = len(terms[0][0])
    tokens, chunk = terms[0][0][0].shape[0] * pieces, terms[0][0][0].shape[1]
    width = weight.shape[1]
    rows = tokens // max(groups, 1)
    count = len(terms) * pieces
    high = min(256, chunk)
    parts = chunk // high
    wanted = ([] if brought else [t[1:] for t in terms]) + [a[1:] for a in ahead]
    streamed = len(wanted) - len(ahead)
    given = len(brought) or 1
    results = max(groups, 1)

    def body(core_ref, *refs):
        w_refs, next_refs, refs = refs[:given], refs[given:][: len(ahead)], refs[given + len(ahead) :]
        copies = []
        if wanted:
            *refs, sems = refs
            if streamed:
                *refs, held = refs
            for n, (side, index) in enumerate(wanted):
                start = place(core_ref, side, index, chunk)
                for r in range(parts):
                    m = n * parts + r
                    here = pl.ds(pl.multiple_of(start + r * high, high), high)
                    if n < streamed:
                        source, target = w_refs[0], held.at[m]
                    else:
                        source = next_refs[n - streamed]
                        target = refs[n - len(wanted)].at[r * high : (r + 1) * high, :]
                    copies.append(pltpu.make_async_copy(source.at[here, :], target, sems.at[m]))
                    copies[-1].start()
        total = refs[count][...] if carried is not None else None
        for n in range(len(terms)):
            left = joined(refs[n * pieces : (n + 1) * pieces])
            for r in range(parts):
                here = slice(r * high, (r + 1) * high)
                if brought:
                    right = w_refs[n][here, :]
                else:
                    copies[n * parts + r].wait()
                    right = held[n * parts + r]
                term = jnp.dot(left[:, here], right, preferred_element_type=F32)
                total = term if total is None else total + term
        outs = refs[count + (carried is not None) :][:results]
        for p, out in enumerate(outs):
            out[...] = total[p * rows : (p + 1) * rows, :].astype(out.dtype)
        for copy in copies[streamed * parts :]:
            copy.wait()

    out_shape = [shape_of((rows, width), BF16 if p else F32) for p in range(results)]
    outs = call(
        body,
        order,
        (list(brought) or [InHbm(weight)])
        + [InHbm(a[0]) for a in ahead]
        + [piece for t in terms for piece in t[0]]
        + ([carried] if carried is not None else []),
        out_shape + [pltpu.VMEM((chunk, width), weight.dtype) for _ in ahead],
        scratch=([pltpu.VMEM((streamed * parts, high, width), BF16)] if streamed else [])
        + ([pltpu.SemaphoreType.DMA((len(wanted) * parts,))] if wanted else []),
    )
    return outs[:results] if groups else outs[0], outs[results:]


def weigh(order, own, others, curvature):
    def body(core_ref, own_ref, *refs):
        total = own_ref[...]
        for other in refs[: len(others)]:
            total += other[...].astype(F32)
        refs[-1][...] = (refs[-2][...] * total).astype(BF16)

    return call(body, order, [own, *others, curvature], shape_of(own.shape, BF16))


def pull_back(order, weighted, weight, added, dtype=BF16):
    def body(core_ref, x_ref, w_ref, *refs):
        total = lax.dot_general(
            x_ref[...], w_ref[...], COLUMNS_BY_COLUMNS, preferred_element_type=F32
        )
        if added is not None:
            total += refs[0][...].astype(F32)
        refs[-1][...] = total.astype(dtype)

    return call(
        body,
        order,
        [weighted, weight] + ([added] if added is not None else []),
        shape_of((weighted.shape[0], weight.shape[0]), dtype),
    )


def cotangents(order, own, others, swish, slope_up, pieces):
    tokens, chunk = own.shape
    high = tokens // pieces

    def body(core_ref, own_ref, *refs):
        back = own_ref[...].astype(F32)
        for other in refs[: len(others)]:
            back += other[...].astype(F32)
        swish_ref, slope_up_ref, *outs = refs[len(others) :]
        for k, by in enumerate((slope_up_ref, swish_ref)):
            term = (back * by[...]).astype(BF16)
            for p, out in enumerate(outs):
                out[k] = term[p * high : (p + 1) * high]

    return call(
        body,
        order,
        [own, *others, swish, slope_up],
        [shape_of((2, high, chunk), BF16)] * pieces,
    )


def outer_down(order, hiddens, weighted, filled):
    tokens, width = weighted.shape
    chunk = hiddens[0][0][0].shape[1]
    count = len(hiddens)
    high = max(chunk // 4, 16)
    parts = chunk // high

    def body(core_ref, *refs):
        x_ref, out, held, sems = refs[count * PIECES :]
        copies = []
        for m, (_, side, index) in enumerate(hiddens):
            hidden = joined(refs[m * PIECES : (m + 1) * PIECES])
            start = place(core_ref, side, index, chunk)
            for r in range(parts):
                n = m * parts + r
                held[n] = lax.dot_general(
                    hidden[:, r * high : (r + 1) * high],
                    x_ref[...],
                    ROWS_BY_ROWS,
                    preferred_element_type=F32,
                ).astype(BF16)
                there = pl.ds(pl.multiple_of(start + r * high, high), high)
                copies.append(
                    pltpu.make_async_copy(held.at[n], out.at[there, :], sems.at[n])
                )
                copies[-1].start()
        for copy in copies:
            copy.wait()

    return call(
        body,
        order,
        [piece for h in hiddens for piece in h[0]] + [weighted],
        [pltpu.HBM((2 * CHUNKS * chunk, width), BF16)],
        scratch=[
            pltpu.VMEM((count * parts, high, width), BF16),
            pltpu.SemaphoreType.DMA((count * parts,)),
        ],
        mib=4 + 2 * count,
        out_specs=[HBM],
        filled=filled,
        marked=True,
    )


def outer_pair(order, rows, terms, hidden_units, filled, marked=True):
    depth, chunk = rows.shape[1], terms[0][0][0].shape[2]
    high = min(256, depth)
    parts = depth // high
    count = len(terms)

    def body(core_ref, x_ref, *refs):
        *pieces, gate_out, up_out, held, sems = refs
        copies, used = [], 0
        for t, (backs, side, index) in enumerate(terms):
            given, used = pieces[used : used + len(backs)], used + len(backs)
            columns = pl.ds(place(core_ref, side, index, chunk), chunk)
            for k, out in enumerate((gate_out, up_out)):
                n = t * 2 + k
                back = jnp.concatenate([ref[k] for ref in given], axis=0)
                for r in range(parts):
                    m = n * parts + r
                    held[m] = lax.dot_general(
                        x_ref[:, r * high : (r + 1) * high],
                        back,
                        ROWS_BY_ROWS,
                        preferred_element_type=F32,
                    ).astype(BF16)
                    copies.append(
                        pltpu.make_async_copy(
                            held.at[m], out.at[r * high : (r + 1) * high, columns], sems.at[m]
                        )
                    )
                    copies[-1].start()
        for copy in copies:
            copy.wait()

    return call(
        body,
        order,
        [rows] + [piece for t in terms for piece in t[0]],
        [pltpu.HBM((depth, hidden_units), BF16)] * 2,
        scratch=[
            pltpu.VMEM((2 * count * parts, high, chunk), BF16),
            pltpu.SemaphoreType.DMA((2 * count * parts,)),
        ],
        mib=6 + 4 * count,
        out_specs=[HBM, HBM],
        filled=filled,
        marked=marked,
    )


def per_device(
    sizes,
    tokens,
    curvature,
    gate_weight,
    up_weight,
    down_weight,
    gate_vector,
    up_vector,
    down_vector,
):
    groups, chips = sizes["dp"], sizes["mp"] // 2
    hidden_units = gate_weight.shape[1]
    group_rows = tokens.shape[0]
    order = Order(lax.rem(lax.axis_index("mp"), 2).astype(jnp.int32)[None])
    mine = lax.dynamic_slice(curvature, (lax.axis_index("dp") * group_rows,), (group_rows,))[:, None]
    def over_dp(value, step):
        return lax.ppermute(value, "dp", [(i, partner(i, step, groups)) for i in range(groups)])

    def back_over_dp(value, step):
        return lax.ppermute(value, "dp", [(i, giver(i, step, groups)) for i in range(groups)])

    def to_all_groups(value):
        return [value] + [over_dp(value, p) for p in reversed(range(1, groups))][::-1]

    def to_core(value):
        return lax.ppermute(value, "mp", [(i, i ^ 1) for i in range(2 * chips)])

    def over_chips(value):
        return [
            lax.ppermute(
                value,
                "mp",
                [(2 * i + c, 2 * partner(i, k, chips) + c) for i in range(chips) for c in range(2)],
            )
            for k in range(1, chips)
        ]

    each = range(CHUNKS)
    primal, probe = (gate_weight, up_weight), (gate_vector, up_vector)
    wanted = [(w, 1, side, i) for side in (1, 0) for i in each for w in primal]
    held = bring(order, wanted[:-2])
    rows = assemble(order, to_all_groups(tokens))
    sent, sums = [], []
    for n in range(0, len(wanted), 2):
        if n == len(held):
            held += bring(order, wanted[-2:])
        weights = [[w] for w in held[n : n + 2]]
        if n < 2 * CHUNKS:
            sent.append(to_core(project(order, rows, weights, [], BF16)[0]))
        else:
            i = len(sums)
            if i == 0:
                (kept,) = project(order, rows, weights, [], F32)
                sums.append(settle(order, kept, sent[i]))
            else:
                sums.append(project(order, rows, weights, [sent[i]], BF16)[0])
    others = [over_chips(s) for s in sums]
    sent = project(order, rows, probe, [], BF16, 3, 1, tuple(each))
    sent = [to_core(piece) for piece in sent]
    held = bring(order, [(w, 1, 0, i) for w in probe for i in each])
    (tangents,) = project(order, rows, [held[:CHUNKS], held[CHUNKS:]], sent, F32)

    acted, carried, tan_others, brought = [], None, [], ()
    for i in each:
        acted.append(activate(order, sums[i], others[i], tangents, i))
        tan_others.append(over_chips(acted[i][0]))
        hidden = (acted[i][3:], 0, i)
        hidden_other = ([to_core(piece) for piece in hidden[0]], 1, i)
        if i < CHUNKS - 1:
            ahead = [(down_vector, side, i + 1) for side in (0, 1)]
        else:
            ahead = [(down_weight, side, 0) for side in (0, 1)]
        carried, brought = contract(
            order, [hidden, hidden_other], down_vector, carried, 0, brought, ahead
        )
        acted[i] = (*acted[i][:3], hidden, hidden_other)
    for i in each:
        last = i == CHUNKS - 1
        hidden_tan = add_up(order, acted[i][0], tan_others[i], 1 if last else PIECES)
        tan_other = [to_core(piece) for piece in hidden_tan]
        terms = [(hidden_tan, 0, i), (tan_other, 1, i)]
        if not last:
            ahead = [(down_weight, 0, i + 1)] if False else []
            carried, brought = contract(order, terms, down_weight, carried, 0, brought, ahead)
        else:
            carried, brought = contract(
                order, terms[:1], down_weight, carried, 0, brought, [(down_weight, 1, i)]
            )
            carried, _ = contract(order, terms[1:], down_weight, carried, groups, brought)
    held = bring(order, [(down_weight, 0, 1, i) for i in each])
    weighted_mine = weigh(
        order, carried[0], [back_over_dp(carried[p], p) for p in reversed(range(1, groups))], mine
    )
    held += bring(order, [(down_weight, 0, 0, i) for i in each])
    weighted = assemble(
        order, to_all_groups(weighted_mine)
    )

    sent = [to_core(pull_back(order, weighted, held[i], None)) for i in each]
    kept = pull_back(order, weighted, held[CHUNKS], None, F32)
    sums = [settle(order, kept, sent[0])]
    sums += [pull_back(order, weighted, held[CHUNKS + i], sent[i]) for i in each[1:]]
    others = [over_chips(s) for s in sums]
    (fisher_down,) = outer_down(
        order, [a[3] for a in acted] + [a[4] for a in acted], weighted, ()
    )
    filled, waiting = (), []
    for i in each:
        backs = cotangents(order, sums[i], others[i], acted[i][1], acted[i][2], BACK_PIECES)
        backs_other = [to_core(piece) for piece in backs]
        filled = outer_pair(order, rows, waiting + [(backs, 0, i)], hidden_units, filled)
        waiting = [(backs_other, 1, i)]
    filled = outer_pair(order, rows, waiting, hidden_units, filled, False)
    return (filled[0], filled[1], fisher_down)


def solution(mesh):
    placed = (
        P(("parts", "dp"), "mp"),
        P("parts"),
        P("mp", "dp"),
        P("mp", "dp"),
        P("dp", "mp"),
        P(("parts", "mp"), "dp"),
        P(("parts", "mp"), "dp"),
        P(("parts", "dp"), "mp"),
    )
    return jax.shard_map(
        functools.partial(per_device, dict(mesh.shape)),
        mesh=mesh,
        in_specs=placed,
        out_specs=(P(("parts", "mp"), "dp"), P(("parts", "mp"), "dp"), P(("parts", "dp"), "mp")),
        check_vma=False,
    )
```
